32 devices in a mesh: grp: 2 (over y), lat: 4 (over z), lon: 4 (over x, core).
Axes of the slice: x: 2, y: 2, z: 4, core: 2. Of those that a mesh axis runs over, the one named last changes fastest.
Arguments:
- state: bfloat16 [2, 64, 512, 512], P('grp', 'lat', 'lon'), may hold values from -6 to 6
- intersection_lists: int32 [2, 4, 4, 3, 16], P('grp', 'lat', 'lon'), may hold values from 0 to 31, as said below
- intersection_matrices: bfloat16 [2, 4, 4, 16, 128, 128], P('grp', 'lat', 'lon'), may hold values from -0.5 to 0.5
- water_indicator: int32 [64, 1024], P('lat', 'lon'), may hold values from 0 to 1, as said below
- atmosphere_kernels: bfloat16 [2, 3, 3, 512, 512], replicated, may hold values from -0.09375 to 0.09375
- ocean_kernels: bfloat16 [2, 3, 3, 256, 256], replicated, may hold values from -0.125 to 0.125
- flux_projection: bfloat16 [512, 256], replicated, may hold values from -0.25 to 0.25
- coupling_matrix: bfloat16 [256, 512], replicated, may hold values from -0.375 to 0.375
Outputs:
- new_state: bfloat16 [2, 64, 512, 512], P('grp', 'lat', 'lon')
The draws below stay inside these ranges and needn't reach their ends.
Inputs may be any that keep to these rules, and one draw needn't show every extreme that they name: intersection_lists[g, i, j] lists the 16 intersections whose source block lies on tile (i, j) of component g (0 atmosphere, 1 ocean). Row 0 is the tile number of the receiving tile of the other component; row 1 the source block, below 16 for atmosphere sources and below 32 for ocean sources; row 2 the receiving block, below 32 on ocean tiles and below 16 on atmosphere tiles. A source tile names one receiving tile at most 2 times, and every source tile names some receiving tile exactly 2 times. `water_indicator`: the share of land differs from tile to tile.
All inputs are finite; a program needn't handle non-finite values.
Results may differ from the reference program's by a relative error of at most 0.01.
Values may be sent and summed in bfloat16 or wider, within the bound.
No kernel may reach another device: no remote copies, remote signals or barrier semaphores. Data moves between devices by JAX's collectives and lax.ppermute only.
A program may use at most 192 MiB of HBM per device.

```python
import jax
import jax.numpy as jnp
from jax import lax

AIR_FEATURES = 512
SEA_FEATURES = 256
PANEL_PARALLELS = 16
PANEL_MERIDIANS = 128
LAYERS = 2
PATCH_PARALLELS = 8
PATCH_MERIDIANS = 16
SLOTS = 2
TILES = 16
ENTRIES = 16
BLOCK = 128
AIR_PATCH_TOTAL = 16
NBO = 32
PARALLEL_LINES = 64
MERIDIAN_TOTAL = 512
N_LAT = 4
N_LON = 4


def one_list(item_key, group_id, list_index):
    slot_total = TILES * SLOTS
    key_perm, key_owner, key_order, key_source, key_target = jax.random.split(item_key, 5)
    scores = jax.random.permutation(key_perm, slot_total)
    forced = jax.random.randint(key_owner, (), 0, TILES)
    forced = jnp.where(list_index == 0, TILES - 1, forced)
    slot_ids = jnp.arange(slot_total)
    scores = jnp.where(slot_ids // SLOTS == forced, slot_ids % SLOTS - SLOTS, scores)
    picked = jnp.argsort(scores, stable=True)[:ENTRIES]
    picked = picked[jax.random.permutation(key_order, ENTRIES)]
    owners = (picked // SLOTS).astype(jnp.int32)
    source_top = jnp.where(group_id == 0, AIR_PATCH_TOTAL, NBO)
    target_top = jnp.where(group_id == 0, NBO, AIR_PATCH_TOTAL)
    sources = jax.random.randint(key_source, (ENTRIES,), 0, source_top)
    targets = jax.random.randint(key_target, (ENTRIES,), 0, target_top)
    sources = sources.at[0].set(source_top - 1)
    targets = targets.at[0].set(0)
    return jnp.stack([owners, sources.astype(jnp.int32), targets.astype(jnp.int32)])


def draw_intersection_lists(key, part):
    keys = jax.random.split(jax.random.fold_in(key, 11), 2 * TILES)
    group_ids = jnp.repeat(jnp.arange(2), TILES)
    list_ids = jnp.arange(2 * TILES)
    lists = jax.vmap(one_list)(keys, group_ids, list_ids)
    return lists.reshape(2, N_LAT, N_LON, 3, ENTRIES).astype(jnp.int32)


def draw_water_indicator(key, part):
    key_tile, key_cell = jax.random.split(jax.random.fold_in(key, 23))
    land_share = jax.random.randint(key_tile, (N_LAT, 1, N_LON, 1), 0, 80)
    draws = jax.random.randint(key_cell, (N_LAT, PANEL_PARALLELS, N_LON, 2 * PANEL_MERIDIANS), 0, 100)
    return (draws >= land_share).astype(jnp.int32).reshape(PARALLEL_LINES, 2 * MERIDIAN_TOTAL)


def steps_of(stream_key, extent, cuts, smallest, largest):
    def one(dim, blocks):
        heights = jax.random.uniform(jax.random.fold_in(jax.random.fold_in(stream_key, 6), dim), (blocks,), jnp.float32, smallest / len(cuts), largest / len(cuts))
        return jnp.repeat(jnp.exp(heights), extent[dim] // blocks).reshape((-1,) + (1,) * (len(extent) - dim - 1))

    level = one(*cuts[0])
    for cut in cuts[1:]:
        level = level * one(*cut)
    return level


def scatter_about(rng, dims, width, limit, cuts=(), dtype=jnp.bfloat16):
    gain = steps_of(rng, dims, cuts, -0.22, 0.18) if cuts else 1.0
    values = jax.random.normal(rng, dims, jnp.float32) * width * gain
    return jnp.minimum(jnp.maximum(values, -limit), limit).astype(dtype)


def setup_inputs(seed: int = 0) -> dict:
    splits = jax.random.split(jax.random.key(seed), 9)
    return {
        "state": scatter_about(splits[0], (2, PARALLEL_LINES, MERIDIAN_TOTAL, AIR_FEATURES), 1.0, 6.0, ((0, 2), (1, 4), (2, 4))),
        "intersection_lists": draw_intersection_lists(jax.random.fold_in(splits[8], 71), 0),
        "intersection_matrices": scatter_about(splits[2], (2, N_LAT, N_LON, ENTRIES, BLOCK, BLOCK), BLOCK ** -0.5, 0.5, ((0, 2), (1, 4), (2, 4))),
        "water_indicator": draw_water_indicator(jax.random.fold_in(splits[8], 71), 0),
        "atmosphere_kernels": scatter_about(splits[4], (LAYERS, 3, 3, AIR_FEATURES, AIR_FEATURES), (9 * AIR_FEATURES) ** -0.5, 0.09375),
        "ocean_kernels": scatter_about(splits[5], (LAYERS, 3, 3, SEA_FEATURES, SEA_FEATURES), (9 * SEA_FEATURES) ** -0.5, 0.125),
        "flux_projection": scatter_about(splits[6], (AIR_FEATURES, SEA_FEATURES), AIR_FEATURES ** -0.5, 0.25),
        "coupling_matrix": scatter_about(splits[7], (SEA_FEATURES, AIR_FEATURES), SEA_FEATURES ** -0.5, 0.375),
    }


def periodic_conv(hidden, kernel):
    patch_span_down, patch_span_across = hidden.shape[0], hidden.shape[1]
    padded = jnp.pad(hidden, ((1, 1), (0, 0), (0, 0)))
    padded = jnp.concatenate([padded[:, -1:], padded, padded[:, :1]], axis=1)
    patch_totals = jnp.zeros((patch_span_down * patch_span_across, kernel.shape[3]), jnp.float32)
    for shift_row in range(3):
        for shift_col in range(3):
            window = padded[shift_row:shift_row + patch_span_down, shift_col:shift_col + patch_span_across].reshape(patch_span_down * patch_span_across, -1)
            patch_totals = patch_totals + jnp.dot(window, kernel[shift_row, shift_col], preferred_element_type=jnp.float32)
    return patch_totals.reshape(patch_span_down, patch_span_across, -1)


def divide_patches(grid_field, tile_rows, tile_cols):
    patch_span_down, patch_span_across, channels = grid_field.shape
    lat_tiles = patch_span_down // tile_rows
    lon_tiles = patch_span_across // tile_cols
    reshaped = grid_field.reshape(lat_tiles, tile_rows // PATCH_PARALLELS, PATCH_PARALLELS, lon_tiles, tile_cols // PATCH_MERIDIANS, PATCH_MERIDIANS, channels)
    reshaped = reshaped.transpose(0, 3, 1, 4, 2, 5, 6)
    return reshaped.reshape(lat_tiles * lon_tiles, (tile_rows // PATCH_PARALLELS) * (tile_cols // PATCH_MERIDIANS), BLOCK, channels)


def assemble_patches(blocks, tile_rows, tile_cols):
    channels = blocks.shape[-1]
    reshaped = blocks.reshape(N_LAT, N_LON, tile_rows // PATCH_PARALLELS, tile_cols // PATCH_MERIDIANS, PATCH_PARALLELS, PATCH_MERIDIANS, channels)
    reshaped = reshaped.transpose(0, 2, 4, 1, 3, 5, 6)
    return reshaped.reshape(N_LAT * tile_rows, N_LON * tile_cols, channels)


def remap_values(source_blocks, label_lookup, remapping_factors, dest_count):
    def one_tile(patch_totals, entry_item):
        blocks, entry_ids, weight = entry_item
        chosen = blocks[entry_ids[1]]
        payload = jnp.einsum("eij,ejk->eik", weight.astype(jnp.float32), chosen.astype(jnp.float32)).astype(jnp.bfloat16)
        patch_totals = patch_totals.at[entry_ids[0], entry_ids[2]].add(payload.astype(jnp.float32))
        return patch_totals, None

    initial = jnp.zeros((TILES, dest_count, BLOCK, SEA_FEATURES), jnp.float32)
    patch_totals, _ = lax.scan(one_tile, initial, (source_blocks, label_lookup, remapping_factors))
    return patch_totals


def reference(state, intersection_lists, intersection_matrices, water_indicator, atmosphere_kernels, ocean_kernels, flux_projection, coupling_matrix):
    atmos = state[0]
    marine_condition = state[1].reshape(PARALLEL_LINES, 2 * MERIDIAN_TOTAL, SEA_FEATURES)
    flux = jnp.dot(atmos.reshape(-1, AIR_FEATURES), flux_projection, preferred_element_type=jnp.float32).astype(jnp.bfloat16)
    flux = flux.reshape(PARALLEL_LINES, MERIDIAN_TOTAL, SEA_FEATURES)
    skin_warmth = marine_condition * water_indicator.astype(jnp.bfloat16)[:, :, None]
    label_lookup = intersection_lists.reshape(2, TILES, 3, ENTRIES)
    remapping_factors = intersection_matrices.reshape(2, TILES, ENTRIES, BLOCK, BLOCK)
    to_ocean = remap_values(divide_patches(flux, PANEL_PARALLELS, PANEL_MERIDIANS), label_lookup[0], remapping_factors[0], NBO)
    deliver_upward = remap_values(divide_patches(skin_warmth, PANEL_PARALLELS, 2 * PANEL_MERIDIANS), label_lookup[1], remapping_factors[1], AIR_PATCH_TOTAL)
    ocean_force = assemble_patches(to_ocean, PANEL_PARALLELS, 2 * PANEL_MERIDIANS)
    skin_warmth_given = assemble_patches(deliver_upward, PANEL_PARALLELS, PANEL_MERIDIANS).astype(jnp.bfloat16)
    air_driving_term = jnp.dot(skin_warmth_given.reshape(-1, SEA_FEATURES), coupling_matrix, preferred_element_type=jnp.float32).reshape(PARALLEL_LINES, MERIDIAN_TOTAL, AIR_FEATURES)
    ocean_mask = water_indicator.astype(jnp.float32)[:, :, None]
    for layer_index in range(LAYERS):
        hidden = jax.nn.silu(atmos.astype(jnp.float32)).astype(jnp.bfloat16)
        update = atmos.astype(jnp.float32) + periodic_conv(hidden, atmosphere_kernels[layer_index])
        if layer_index == 0:
            update = update + air_driving_term
        atmos = update.astype(jnp.bfloat16)
        hidden = jax.nn.silu(marine_condition.astype(jnp.float32)).astype(jnp.bfloat16)
        update = marine_condition.astype(jnp.float32) + periodic_conv(hidden, ocean_kernels[layer_index])
        if layer_index == 0:
            update = update + ocean_force
        marine_condition = (update * ocean_mask).astype(jnp.bfloat16)
    return jnp.stack([atmos, marine_condition.reshape(PARALLEL_LINES, MERIDIAN_TOTAL, AIR_FEATURES)])
```

```python
import functools

import jax
import jax.numpy as jnp
from jax import lax
from jax.experimental import pallas as pl
from jax.experimental.pallas import tpu as pltpu
from jax.sharding import PartitionSpec as P

LAYERS = 2
BLOCK_ROWS = 8
BLOCK_COLS = 16
BLOCK = BLOCK_ROWS * BLOCK_COLS
SLOTS = 2
HALF = BLOCK // 2
HALF_ROWS = BLOCK_ROWS // 2
VMEM_BYTES = 48 * 2**20

F32 = jnp.float32
BF16 = jnp.bfloat16

VMEM = pl.BlockSpec(memory_space=pltpu.VMEM)
SMEM = pl.BlockSpec(memory_space=pltpu.SMEM)
ANY = pl.BlockSpec(memory_space=pl.ANY)


def silu(v):
    return v / (1.0 + jnp.exp(-v))


def iota(shape, dim):
    return lax.broadcasted_iota(jnp.int32, shape, dim)


def dot(a, b):
    return jnp.dot(a, b, preferred_element_type=F32)


def params(**kwargs):
    return pltpu.CompilerParams(vmem_limit_bytes=VMEM_BYTES, **kwargs)


def on_ocean():
    return lax.axis_index("grp") == 1


def fill_water(water_ref, turned_ref):
    count, cols = water_ref.shape
    turned_ref[:, 0:count] = water_ref[...].astype(F32).T


def water_of_row(turned_ref, rows, r, width, start, size):
    parts = [
        jnp.broadcast_to(turned_ref[start : start + size, p * rows + r : p * rows + r + 1], (size, width))
        for p in range(2)
    ]
    return jnp.concatenate(parts, axis=1)


def payload_kernel(
    lists_ref, state_ref, matrices_ref, water_ref, flux_ref, first_ref, second_ref, flux, surface, turned, count
):
    rows, cols, width = state_ref.shape
    half = width // 2
    entries = matrices_ref.shape[0]
    tiles = first_ref.shape[0] // SLOTS
    ocean = on_ocean()

    def clear(t, _):
        count[t] = 0
        return 0

    lax.fori_loop(0, tiles, clear, 0)
    i = iota((BLOCK, BLOCK), 0)
    j = iota((BLOCK, BLOCK), 1)

    def put(e, payload):
        owner = lists_ref[0, e]
        rank = count[owner]
        count[owner] = rank + 1
        slot = owner * SLOTS + rank
        first_ref[slot] = payload[:HALF]
        second_ref[slot] = payload[HALF:]

    @pl.when(jnp.logical_not(ocean))
    def _():
        p, r, c = (i // 32) % 2, (i // 64) * 4 + (i // 8) % 4, i % 8
        turn = (j == r * BLOCK_COLS + 2 * c + p).astype(BF16)
        step = 4
        for r0 in range(0, rows, step):
            block = state_ref[r0 : r0 + step].reshape(step * cols, width)
            flux[r0 : r0 + step] = dot(block, flux_ref[...]).astype(BF16).reshape(step, cols, half)
        across = cols // BLOCK_COLS

        def entry(e, _):
            source = lists_ref[1, e]
            r0 = (source // across) * BLOCK_ROWS
            c0 = pl.multiple_of((source % across) * BLOCK_COLS, BLOCK_COLS)
            chosen = flux[pl.ds(r0, BLOCK_ROWS), pl.ds(c0, BLOCK_COLS), :].reshape(BLOCK, half)
            weight = dot(turn, matrices_ref[e]).astype(BF16)
            put(e, dot(weight, chosen).astype(BF16))
            return 0

        lax.fori_loop(0, entries, entry, 0, unroll=2)

    @pl.when(ocean)
    def _():
        p, r, c = j // 64, (j // 8) % 8, j % 8
        turn = (i == r * BLOCK_COLS + 2 * c + p).astype(BF16)
        fill_water(water_ref, turned)
        for r0 in range(rows):
            surface[r0] = state_ref[r0].astype(F32) * water_of_row(turned, rows, r0, half, 0, cols)
        wide = BLOCK_COLS // 2
        across = cols // wide

        def entry(e, _):
            source = lists_ref[1, e]
            r0 = (source // across) * BLOCK_ROWS
            c0 = pl.multiple_of((source % across) * wide, wide)
            block = surface[pl.ds(r0, BLOCK_ROWS), pl.ds(c0, wide), :]
            chosen = jnp.concatenate(
                [block[:, :, q * half : (q + 1) * half].reshape(BLOCK // 2, half) for q in range(2)], axis=0
            ).astype(BF16)
            weight = dot(matrices_ref[e], turn).astype(BF16)
            put(e, dot(weight, chosen).astype(BF16))
            return 0

        lax.fori_loop(0, entries, entry, 0, unroll=2)


def payloads(lists, state, matrices, water, flux_projection, tiles):
    rows, cols, width = state.shape
    half = width // 2
    slots = jax.ShapeDtypeStruct((tiles * SLOTS, HALF, half), BF16)
    return pl.pallas_call(
        payload_kernel,
        out_shape=(slots, slots),
        in_specs=[SMEM, VMEM, VMEM, VMEM, VMEM],
        out_specs=(VMEM, VMEM),
        scratch_shapes=[
            pltpu.VMEM((rows, cols, half), BF16),
            pltpu.VMEM((rows, cols, width), F32),
            pltpu.VMEM((cols, 128), F32),
            pltpu.SMEM((tiles,), jnp.int32),
        ],
        compiler_params=params(),
        name="payload",
    )(lists, state, matrices, water, flux_projection)


GROUP = 4


def weight_copies(layer, kernels_ref, held, sems):
    return [
        pltpu.make_async_copy(kernels_ref.at[layer, d], held.at[d], sems.at[d]) for d in range(3)
    ]


def set_columns(line, before, after):
    cols = line.shape[0]
    at = iota(line.shape, 0)
    left = jnp.where(at == 0, before, pltpu.roll(line, 1, 0))
    right = jnp.where(at == cols - 1, after, pltpu.roll(line, cols - 1, 0))
    return left, right


def air_line(h, before, after):
    left, right = set_columns(h, before, after)
    return jnp.concatenate([left, h, right], axis=1).astype(BF16)


def sea_line(h, before, after):
    half = h.shape[1] // 2
    left, _ = set_columns(h[:, half:], before[:, half:], after[:, half:])
    _, right = set_columns(h[:, :half], before[:, :half], after[:, :half])
    return jnp.concatenate([left, h, right], axis=1).astype(BF16)


def air_product(block, kernel):
    return dot(block, kernel.reshape(-1, kernel.shape[-1]))


def sea_product(block, kernel):
    width = kernel.shape[-1]
    flat = kernel.reshape(-1, width)
    return jnp.concatenate(
        [dot(block[:, : 3 * width], flat), dot(block[:, width : 4 * width], flat)], axis=1
    )


def conv_kernel(layer, halo, *refs):
    if halo:
        (x_ref, top_ref, bottom_ref, left_ref, right_ref, air_ref, sea_ref, sum_ref) = refs[:8]
        (lined, air_held, sea_held, sems) = refs[8:]
    else:
        (x_ref, water_ref, air_ref, sea_ref, out_ref, lines_ref, sides_ref) = refs[:7]
        (lined, air_held, sea_held, turned, sems) = refs[7:]
    rows, cols, width = x_ref.shape
    half = width // 2
    ocean = on_ocean()

    def run(kernels_ref, held, make_line, product, masked):
        copies = weight_copies(layer, kernels_ref, held, sems)
        for copy in copies:
            copy.start()
        wide = 3 * width if not masked else 2 * width
        none = jnp.zeros((1, width), F32)

        def put(r, line, before, after):
            lined[r, :, 0:wide] = make_line(silu(line.astype(F32)), before, after)

        if halo:
            before_all = silu(left_ref[...].astype(F32))
            after_all = silu(right_ref[...].astype(F32))
            for r in range(rows + 2):
                line = top_ref[...] if r == 0 else bottom_ref[...] if r == rows + 1 else x_ref[r - 1]
                put(r, line, before_all[r : r + 1], after_all[r : r + 1])
        else:
            for r in (0, rows + 1):
                lined[r, :, 0:wide] = jnp.zeros((cols, wide), BF16)
            for r in range(rows):
                put(r + 1, x_ref[r], none, none)
        for copy in copies:
            copy.wait()
        if masked and not halo:
            fill_water(water_ref, turned)

        def products(r0):
            total = x_ref[pl.ds(r0, GROUP)].astype(F32).reshape(GROUP * cols, width)
            for d in range(3):
                block = lined[pl.ds(r0 + d, GROUP), :, 0:wide].reshape(GROUP * cols, wide)
                total = total + product(block, held[d])
            return total.reshape(GROUP, cols, width)

        if halo:

            @pl.loop(0, rows // GROUP)
            def _(g):
                sum_ref[pl.ds(g * GROUP, GROUP)] = products(g * GROUP)
        else:
            for r0 in range(0, rows, GROUP):
                total = products(r0)
                for k in range(GROUP):
                    r = r0 + k
                    if r == 0 or r == rows - 1:
                        lines_ref[0 if r == 0 else 1] = total[k]
                    sides_ref[0, r] = total[k, :BLOCK_COLS]
                    sides_ref[1, r] = total[k, cols - BLOCK_COLS :]
                    line = total[k]
                    if masked:
                        line = line * water_of_row(turned, rows, r, half, 0, cols)
                    out_ref[r] = line.astype(BF16)

    @pl.when(jnp.logical_not(ocean))
    def _():
        run(air_ref, air_held, air_line, air_product, False)

    @pl.when(ocean)
    def _():
        run(sea_ref, sea_held, sea_line, sea_product, True)


def conv_scratch(state, air_kernels, sea_kernels):
    rows, cols, width = state.shape
    return [
        pltpu.VMEM((rows + 2, cols, 3 * width), BF16),
        pltpu.VMEM(air_kernels.shape[1:], BF16),
        pltpu.VMEM(sea_kernels.shape[1:], BF16),
    ]


def conv_cost(state, air_kernels):
    cells = state.shape[0] * state.shape[1]
    width = state.shape[2]
    return pl.CostEstimate(
        flops=2 * 9 * cells * width * width,
        bytes_accessed=air_kernels[0].size * 2 + state.size * 6,
        transcendentals=state.size,
    )


def conv_with_halo(layer, state, halo, air_kernels, sea_kernels):
    return pl.pallas_call(
        functools.partial(conv_kernel, layer, True),
        out_shape=jax.ShapeDtypeStruct(state.shape, F32),
        in_specs=[VMEM] * 5 + [ANY] * 2,
        out_specs=VMEM,
        scratch_shapes=conv_scratch(state, air_kernels, sea_kernels) + [pltpu.SemaphoreType.DMA((3,))],
        compiler_params=params(),
        cost_estimate=conv_cost(state, air_kernels),
        name="conv_halo",
    )(state, *halo, air_kernels, sea_kernels)


def conv_inside(layer, state, water, air_kernels, sea_kernels):
    rows, cols, width = state.shape
    return pl.pallas_call(
        functools.partial(conv_kernel, layer, False),
        out_shape=(
            jax.ShapeDtypeStruct(state.shape, BF16),
            jax.ShapeDtypeStruct((2, cols, width), F32),
            jax.ShapeDtypeStruct((2, rows, BLOCK_COLS, width), F32),
        ),
        in_specs=[VMEM] * 2 + [ANY] * 2,
        out_specs=(VMEM,) * 3,
        scratch_shapes=conv_scratch(state, air_kernels, sea_kernels)
        + [pltpu.VMEM((cols, 128), F32), pltpu.SemaphoreType.DMA((3,))],
        compiler_params=params(),
        cost_estimate=conv_cost(state, air_kernels),
        name="conv_inside",
    )(state, water, air_kernels, sea_kernels)


def edge_kernel(
    layer,
    out_in_ref,
    lines_ref,
    sides_ref,
    top_ref,
    bottom_ref,
    left_ref,
    right_ref,
    water_ref,
    air_ref,
    sea_ref,
    out_ref,
    air_held,
    sea_held,
    turned,
    line_out,
    side_out,
    sems,
    out_sems,
):
    del out_in_ref
    _, rows, _, width = sides_ref.shape
    cols = lines_ref.shape[1]
    half = width // 2
    ocean = on_ocean()

    def run(kernels_ref, held, make_line, product, masked):
        copies = weight_copies(layer, kernels_ref, held, sems)
        for copy in copies:
            copy.start()
        none = jnp.zeros((1, width), F32)
        top = make_line(silu(top_ref[...].astype(F32)), none, none)
        bottom = make_line(silu(bottom_ref[...].astype(F32)), none, none)
        before = silu(left_ref[...].astype(F32))
        after = silu(right_ref[...].astype(F32))
        if masked:
            before, after = before[:, half:], after[:, :half]
            fill_water(water_ref, turned)
        size = before.shape[1]
        for copy in copies:
            copy.wait()
        west = jnp.zeros((rows, size), F32)
        east = jnp.zeros((rows, size), F32)
        for d in range(3):
            west = west + dot(before[d : d + rows].astype(BF16), held[d, 0])
            east = east + dot(after[d : d + rows].astype(BF16), held[d, 2])
        if masked:
            blank = jnp.zeros((rows, half), F32)
            west = jnp.concatenate([west, blank], axis=1)
            east = jnp.concatenate([blank, east], axis=1)

        def finish(value, r, start, size):
            if masked:
                value = value * water_of_row(turned, rows, r, half, start, size)
            return value.astype(BF16)

        at = iota((cols, width), 0)
        for k, (line, d) in enumerate(((top, 0), (bottom, 2))):
            r = 0 if k == 0 else rows - 1
            total = lines_ref[k] + product(line, held[d])
            total = total + jnp.where(at == 0, west[r : r + 1], 0.0)
            total = total + jnp.where(at == cols - 1, east[r : r + 1], 0.0)
            line_out[k] = finish(total, r, 0, cols)
        at = iota((BLOCK_COLS, width), 0)
        for r in range(1, rows - 1):
            total = sides_ref[0, r] + jnp.where(at == 0, west[r : r + 1], 0.0)
            side_out[0, r - 1] = finish(total, r, 0, BLOCK_COLS)
            total = sides_ref[1, r] + jnp.where(at == BLOCK_COLS - 1, east[r : r + 1], 0.0)
            side_out[1, r - 1] = finish(total, r, cols - BLOCK_COLS, BLOCK_COLS)

    @pl.when(jnp.logical_not(ocean))
    def _():
        run(air_ref, air_held, air_line, air_product, False)

    @pl.when(ocean)
    def _():
        run(sea_ref, sea_held, sea_line, sea_product, True)

    inner = pl.ds(1, rows - 2)
    copies = [
        pltpu.make_async_copy(line_out.at[0], out_ref.at[0], out_sems.at[0]),
        pltpu.make_async_copy(line_out.at[1], out_ref.at[rows - 1], out_sems.at[1]),
        pltpu.make_async_copy(side_out.at[0], out_ref.at[inner, pl.ds(0, BLOCK_COLS)], out_sems.at[2]),
        pltpu.make_async_copy(
            side_out.at[1], out_ref.at[inner, pl.ds(cols - BLOCK_COLS, BLOCK_COLS)], out_sems.at[3]
        ),
    ]
    for copy in copies:
        copy.start()
    for copy in copies:
        copy.wait()


def fix_edges(layer, out, lines, sides, halo, water, air_kernels, sea_kernels):
    rows, cols, width = out.shape
    return pl.pallas_call(
        functools.partial(edge_kernel, layer),
        out_shape=jax.ShapeDtypeStruct(out.shape, BF16),
        in_specs=[ANY] + [VMEM] * 7 + [ANY] * 2,
        out_specs=ANY,
        scratch_shapes=[
            pltpu.VMEM(air_kernels.shape[1:], BF16),
            pltpu.VMEM(sea_kernels.shape[1:], BF16),
            pltpu.VMEM((cols, 128), F32),
            pltpu.VMEM((2, cols, width), BF16),
            pltpu.VMEM((2, rows - 2, BLOCK_COLS, width), BF16),
            pltpu.SemaphoreType.DMA((3,)),
            pltpu.SemaphoreType.DMA((4,)),
        ],
        input_output_aliases={0: 0},
        compiler_params=params(),
        name="fix_edges",
    )(out, lines, sides, *halo, water, air_kernels, sea_kernels)


def update_kernel(
    labels_ref,
    first_ref,
    second_ref,
    sum_hbm,
    water_ref,
    coupling_ref,
    new_ref,
    top_ref,
    bottom_ref,
    left_ref,
    right_ref,
    total,
    sum_ref,
    turned,
    sems,
):
    rows, cols, width = new_ref.shape
    half = width // 2
    tiles = first_ref.shape[0] // SLOTS
    ocean = on_ocean()
    me = lax.axis_index("lat") * lax.axis_size("lon") + lax.axis_index("lon")
    quarter = rows // 4
    copies = [
        pltpu.make_async_copy(
            sum_hbm.at[pl.ds(k * quarter, quarter)], sum_ref.at[pl.ds(k * quarter, quarter)], sems.at[k]
        )
        for k in range(4)
    ]
    for copy in copies:
        copy.start()

    def gather(add):
        def slot(s, _):
            label = labels_ref[(jnp.bitwise_xor(s // SLOTS, me)) * SLOTS + s % SLOTS]

            @pl.when(label >= 0)
            def _():
                add(s, label)

            return 0

        lax.fori_loop(0, tiles * SLOTS, slot, 0)

    def store(r, line):
        low = line.astype(BF16)
        new_ref[r] = low
        exact = low.astype(F32)
        left_ref[r : r + 1] = exact[0:1]
        right_ref[r : r + 1] = exact[cols - 1 : cols]
        if r == 0:
            top_ref[...] = low
        if r == rows - 1:
            bottom_ref[...] = low

    @pl.when(jnp.logical_not(ocean))
    def _():
        total[:, :, 0:half] = jnp.zeros((rows, cols, half), F32)
        across = cols // BLOCK_COLS

        def add(s, label):
            r0 = (label // across) * BLOCK_ROWS
            c0 = pl.multiple_of((label % across) * BLOCK_COLS, BLOCK_COLS)
            for h, ref in enumerate((first_ref, second_ref)):
                value = ref[s].astype(F32).reshape(HALF_ROWS, BLOCK_COLS, half)
                total[pl.ds(r0 + h * HALF_ROWS, HALF_ROWS), pl.ds(c0, BLOCK_COLS), 0:half] += value

        gather(add)
        for k in range(4):
            r0 = k * quarter
            block = total[r0 : r0 + quarter, :, 0:half].astype(BF16).reshape(quarter * cols, half)
            force = dot(block, coupling_ref[...]).reshape(quarter, cols, width)
            copies[k].wait()
            for q in range(quarter):
                store(r0 + q, sum_ref[r0 + q] + force[q])

    @pl.when(ocean)
    def _():
        total[...] = jnp.zeros_like(total)
        fill_water(water_ref, turned)
        wide = BLOCK_COLS // 2
        across = cols // wide

        def add(s, label):
            r0 = (label // across) * BLOCK_ROWS
            c0 = pl.multiple_of((label % across) * wide, wide)
            for h, ref in enumerate((first_ref, second_ref)):
                value = ref[s].astype(F32).reshape(2, HALF_ROWS, wide, half)
                for p in range(2):
                    total[
                        pl.ds(r0 + h * HALF_ROWS, HALF_ROWS), pl.ds(c0, wide), p * half : (p + 1) * half
                    ] += value[p]

        gather(add)
        for k in range(4):
            copies[k].wait()
            for q in range(quarter):
                r = k * quarter + q
                store(r, (sum_ref[r] + total[r]) * water_of_row(turned, rows, r, half, 0, cols))


def update(labels, first, second, summed, water, coupling_matrix):
    rows, cols, width = summed.shape
    return pl.pallas_call(
        update_kernel,
        out_shape=(
            jax.ShapeDtypeStruct((rows, cols, width), BF16),
            jax.ShapeDtypeStruct((cols, width), BF16),
            jax.ShapeDtypeStruct((cols, width), BF16),
            jax.ShapeDtypeStruct((rows, width), F32),
            jax.ShapeDtypeStruct((rows, width), F32),
        ),
        in_specs=[SMEM, VMEM, VMEM, ANY, VMEM, VMEM],
        out_specs=(VMEM,) * 5,
        scratch_shapes=[
            pltpu.VMEM((rows, cols, width), F32),
            pltpu.VMEM((rows, cols, width), F32),
            pltpu.VMEM((cols, 128), F32),
            pltpu.SemaphoreType.DMA((4,)),
        ],
        compiler_params=params(),
        name="update",
    )(labels, first, second, summed, water, coupling_matrix)


def exchange(value, axis, bit):
    return lax.ppermute(value, axis, [(i, i ^ bit) for i in range(lax.axis_size(axis))])


def across_groups(value):
    return exchange(value, "grp", 1)


def to_owners(value):
    return lax.all_to_all(value, ("lat", "lon"), split_axis=0, concat_axis=0, tiled=True)


def all_lists(lists):
    held = across_groups(lists)[None]
    for axis in ("lon", "lat"):
        bit = 1
        while bit < lax.axis_size(axis):
            held = jnp.concatenate([held, exchange(held, axis, bit)], axis=0)
            bit *= 2
    return held


def slot_labels(held):
    me = lax.axis_index("lat") * lax.axis_size("lon") + lax.axis_index("lon")
    mine = (held[:, 0] == me).astype(jnp.int32)
    rank = jnp.cumsum(mine, axis=1) - mine
    labels = [
        jnp.sum(mine * (rank == slot) * (held[:, 2] + 1), axis=1) - 1 for slot in range(SLOTS)
    ]
    return jnp.stack(labels, axis=1).reshape(-1)


def halo_of(top, bottom, left, right):
    lats, lons = lax.axis_size("lat"), lax.axis_size("lon")
    down = [(i, i + 1) for i in range(lats - 1)]
    up = [(i + 1, i) for i in range(lats - 1)]
    east = [(i, (i + 1) % lons) for i in range(lons)]
    west = [((i + 1) % lons, i) for i in range(lons)]
    above = lax.ppermute(bottom, "lat", down)
    below = lax.ppermute(top, "lat", up)
    first = jnp.concatenate([above[:1], left.astype(BF16), below[:1]], axis=0)
    last = jnp.concatenate([above[-1:], right.astype(BF16), below[-1:]], axis=0)
    before = lax.ppermute(last, "lon", east)
    after = lax.ppermute(first, "lon", west)
    return above, below, before, after


def body(
    state,
    intersection_lists,
    intersection_matrices,
    water_indicator,
    atmosphere_kernels,
    ocean_kernels,
    flux_projection,
    coupling_matrix,
):
    current = state[0]
    rows, cols, width = current.shape
    tiles = lax.axis_size("lat") * lax.axis_size("lon")
    entries = intersection_lists.shape[-1]
    lists = intersection_lists.reshape(3, entries)
    matrices = intersection_matrices.reshape(entries, BLOCK, BLOCK)
    water = water_indicator.reshape(rows, cols, 2).transpose(2, 0, 1).reshape(2 * rows, cols)

    first, second = payloads(lists, current, matrices, water, flux_projection, tiles)
    first = across_groups(first)
    second = to_owners(second)
    first = to_owners(first)
    second = across_groups(second)
    labels = slot_labels(all_lists(lists))

    halo = halo_of(current[0], current[-1], current[:, 0], current[:, -1])
    summed = conv_with_halo(0, current, halo, atmosphere_kernels, ocean_kernels)
    current, *rim = update(labels, first, second, summed, water, coupling_matrix)
    for layer in range(1, LAYERS):
        halo = halo_of(*rim)
        out, lines, sides = conv_inside(layer, current, water, atmosphere_kernels, ocean_kernels)
        current = fix_edges(layer, out, lines, sides, halo, water, atmosphere_kernels, ocean_kernels)
    return current[None]


def solution(mesh):
    placed = (
        P("grp", "lat", "lon", None),
        P("grp", "lat", "lon", None, None),
        P("grp", "lat", "lon", None, None, None),
        P("lat", "lon"),
        P(),
        P(),
        P(),
        P(),
    )
    return jax.shard_map(
        body, mesh=mesh, in_specs=placed, out_specs=P("grp", "lat", "lon", None), check_vma=False
    )
```

```python
import functools

import jax
import jax.numpy as jnp
from jax import lax
from jax.experimental import pallas as pl
from jax.experimental.pallas import tpu as pltpu
from jax.sharding import PartitionSpec as P

BLOCK_ROWS = 8
BLOCK_COLS = 16
BLOCK = BLOCK_ROWS * BLOCK_COLS
SLOTS = 2
HALF = BLOCK // 2
HALF_ROWS = BLOCK_ROWS // 2
VMEM_BYTES = 28 * 2**20

F32 = jnp.float32
BF16 = jnp.bfloat16

VMEM = pl.BlockSpec(memory_space=pltpu.VMEM)
SMEM = pl.BlockSpec(memory_space=pltpu.SMEM)
HBM = pl.BlockSpec(memory_space=pltpu.HBM)


def silu(v):
    return v / (1.0 + jnp.exp(-v))


def iota(shape, dim):
    return lax.broadcasted_iota(jnp.int32, shape, dim)


def dot(a, b):
    return jnp.dot(a, b, preferred_element_type=F32)


def params(**kwargs):
    return pltpu.CompilerParams(vmem_limit_bytes=VMEM_BYTES, **kwargs)


def on_ocean():
    return lax.axis_index("grp") == 1


def fill_water(water_ref, wide_ref, turned_ref):
    rows, longitudes = water_ref.shape
    wide_ref[:, 0:rows] = water_ref[...].astype(F32).T
    for p in range(2):
        turned_ref[:, p * rows : (p + 1) * rows] = wide_ref[pl.ds(p, longitudes // 2, stride=2), :][:, 0:rows]


def water_scratch(cols):
    return [pltpu.VMEM((2 * cols, 128), F32), pltpu.VMEM((cols, 128), F32)]


def water_of_row(turned_ref, rows, r, width, start, size):
    parts = [
        jnp.broadcast_to(turned_ref[start : start + size, p * rows + r : p * rows + r + 1], (size, width))
        for p in range(2)
    ]
    return jnp.concatenate(parts, axis=1)


def rim_shapes(rows, cols, width):
    line = jax.ShapeDtypeStruct((cols, width), BF16)
    side = jax.ShapeDtypeStruct((rows, width), F32)
    return (line, line, side, side)


def put_rim(rim, r, rows, line):
    top_ref, bottom_ref, left_ref, right_ref = rim
    cols = line.shape[0]
    exact = line.astype(F32)
    left_ref[r : r + 1] = exact[0:1]
    right_ref[r : r + 1] = exact[cols - 1 : cols]
    if r == 0:
        top_ref[...] = line
    if r == rows - 1:
        bottom_ref[...] = line


def payload_kernel(
    lists_ref, state_hbm, matrices_hbm, water_ref, flux_hbm,
    first_ref, second_ref, lists_out, top_ref, bottom_ref, left_ref, right_ref,
    state_ref, matrices_ref, flux_ref, flux, surface, wide_water, turned, count, sems,
):
    rows, cols, width = state_ref.shape
    half = width // 2
    entries = matrices_ref.shape[0]
    tiles = second_ref.shape[0] // SLOTS
    ocean = on_ocean()
    pieces = 4
    step = rows // pieces
    flux_copy = pltpu.make_async_copy(flux_hbm, flux_ref, sems.at[pieces])
    matrices_copy = pltpu.make_async_copy(matrices_hbm, matrices_ref, sems.at[pieces + 1])
    state_copies = [
        pltpu.make_async_copy(state_hbm.at[pl.ds(k * step, step)], state_ref.at[pl.ds(k * step, step)], sems.at[k])
        for k in range(pieces)
    ]
    flux_copy.start()
    for copy in state_copies:
        copy.start()
    matrices_copy.start()

    def clear(t, _):
        count[t] = 0
        return 0

    lax.fori_loop(0, tiles, clear, 0)

    def keep(e, _):
        for k in range(3):
            lists_out[k, e] = lists_ref[k, e]
        return 0

    lax.fori_loop(0, entries, keep, 0)
    i = iota((BLOCK, BLOCK), 0)
    j = iota((BLOCK, BLOCK), 1)

    def put(e, payload):
        owner = lists_ref[0, e]
        rank = count[owner]
        count[owner] = rank + 1
        first_ref[e] = payload[:HALF]
        second_ref[owner * SLOTS + rank] = payload[HALF:]

    flux_copy.wait()

    @pl.when(jnp.logical_not(ocean))
    def _():
        p, r, c = (i // 32) % 2, (i // 64) * 4 + (i // 8) % 4, i % 8
        turn = (j == r * BLOCK_COLS + 2 * c + p).astype(BF16)
        for k in range(pieces):
            state_copies[k].wait()
            block = state_ref[k * step : (k + 1) * step].reshape(step * cols, width)
            flux[k * step : (k + 1) * step] = (
                dot(block, flux_ref[...]).astype(BF16).reshape(step, cols, half)
            )
        matrices_copy.wait()
        across = cols // BLOCK_COLS

        def entry(e, _):
            source = lists_ref[1, e]
            r0 = (source // across) * BLOCK_ROWS
            c0 = pl.multiple_of((source % across) * BLOCK_COLS, BLOCK_COLS)
            chosen = flux[pl.ds(r0, BLOCK_ROWS), pl.ds(c0, BLOCK_COLS), :].reshape(BLOCK, half)
            weight = dot(turn, matrices_ref[e]).astype(BF16)
            put(e, dot(weight, chosen).astype(BF16))
            return 0

        lax.fori_loop(0, entries, entry, 0, unroll=8)

    @pl.when(ocean)
    def _():
        p, r, c = j // 64, (j // 8) % 8, j % 8
        turn = (i == r * BLOCK_COLS + 2 * c + p).astype(BF16)
        fill_water(water_ref, wide_water, turned)
        for k in range(pieces):
            state_copies[k].wait()
            for r0 in range(k * step, (k + 1) * step):
                surface[r0] = state_ref[r0].astype(F32) * water_of_row(turned, rows, r0, half, 0, cols)
        matrices_copy.wait()
        wide = BLOCK_COLS // 2
        across = cols // wide

        def entry(e, _):
            source = lists_ref[1, e]
            r0 = (source // across) * BLOCK_ROWS
            c0 = pl.multiple_of((source % across) * wide, wide)
            block = surface[pl.ds(r0, BLOCK_ROWS), pl.ds(c0, wide), :]
            chosen = jnp.concatenate(
                [block[:, :, q * half : (q + 1) * half].reshape(BLOCK // 2, half) for q in range(2)], axis=0
            ).astype(BF16)
            weight = dot(matrices_ref[e], turn).astype(BF16)
            put(e, dot(weight, chosen).astype(BF16))
            return 0

        lax.fori_loop(0, entries, entry, 0, unroll=8)

    for r in range(rows):
        put_rim((top_ref, bottom_ref, left_ref, right_ref), r, rows, state_ref[r])


def payloads(lists, state, matrices, water, flux_projection, tiles):
    rows, cols, width = state.shape
    half = width // 2
    entries = lists.shape[1]
    return pl.pallas_call(
        payload_kernel,
        out_shape=(
            jax.ShapeDtypeStruct((entries, HALF, half), BF16),
            jax.ShapeDtypeStruct((tiles * SLOTS, HALF, half), BF16),
            jax.ShapeDtypeStruct(lists.shape, jnp.int32),
        )
        + rim_shapes(rows, cols, width),
        in_specs=[SMEM, HBM, HBM, VMEM, HBM],
        out_specs=(VMEM, VMEM, SMEM) + (VMEM,) * 4,
        scratch_shapes=[
            pltpu.VMEM(state.shape, BF16),
            pltpu.VMEM(matrices.shape, BF16),
            pltpu.VMEM(flux_projection.shape, BF16),
            pltpu.VMEM((rows, cols, half), BF16),
            pltpu.VMEM((rows, cols, width), F32),
        ]
        + water_scratch(cols)
        + [pltpu.SMEM((tiles,), jnp.int32), pltpu.SemaphoreType.DMA((6,))],
        compiler_params=params(),
        name="payload",
    )(lists, state, matrices, water, flux_projection)


def pack_kernel(
    lists_ref, dense_ref, above_ref, below_ref, left_ref, right_ref,
    slots_ref, labels_ref, west_ref, east_ref, count,
):
    tiles, _, entries = lists_ref.shape
    rows = left_ref.shape[0]
    cols = above_ref.shape[0]
    me = lax.axis_index("lat") * lax.axis_size("lon") + lax.axis_index("lon")

    def clear(t, _):
        count[t] = 0
        for slot in range(SLOTS):
            labels_ref[t * SLOTS + slot] = -1
        return 0

    lax.fori_loop(0, tiles, clear, 0)

    def place(e, _):
        owner = lists_ref[0, 0, e]
        rank = count[owner]
        count[owner] = rank + 1
        slots_ref[owner * SLOTS + rank] = dense_ref[e]
        return 0

    lax.fori_loop(0, entries, place, 0)

    def source(t, _):
        def entry(e, rank):
            hit = lists_ref[t, 0, e] == me

            @pl.when(hit)
            def _():
                labels_ref[jnp.bitwise_xor(t, me) * SLOTS + rank] = lists_ref[t, 2, e]

            return rank + hit.astype(jnp.int32)

        lax.fori_loop(0, entries, entry, 0, unroll=8)
        return 0

    lax.fori_loop(0, tiles, source, 0)
    side_message(above_ref, below_ref, left_ref, right_ref, west_ref, east_ref, rows, cols)


def side_message(above_ref, below_ref, left_ref, right_ref, west_ref, east_ref, rows, cols):
    for ref, side, at in ((west_ref, left_ref, 0), (east_ref, right_ref, cols - 1)):
        ref[0:1] = above_ref[at : at + 1].astype(F32)
        ref[1 : rows + 1] = side[...]
        ref[rows + 1 : rows + 2] = below_ref[at : at + 1].astype(F32)


def pack(held, dense, above, below, left, right):
    tiles = held.shape[0]
    rows, width = left.shape
    side = jax.ShapeDtypeStruct((rows + 2, width), F32)
    return pl.pallas_call(
        pack_kernel,
        out_shape=(
            jax.ShapeDtypeStruct((tiles * SLOTS,) + dense.shape[1:], BF16),
            jax.ShapeDtypeStruct((tiles * SLOTS,), jnp.int32),
            side,
            side,
        ),
        in_specs=[SMEM] + [VMEM] * 5,
        out_specs=(VMEM, SMEM, VMEM, VMEM),
        scratch_shapes=[pltpu.SMEM((tiles,), jnp.int32)],
        compiler_params=params(),
        name="pack",
    )(held, dense, above, below, left, right)


GROUP = 4


def set_columns(line, before, after):
    cols = line.shape[0]
    at = iota(line.shape, 0)
    left = jnp.where(at == 0, before, pltpu.roll(line, 1, 0))
    right = jnp.where(at == cols - 1, after, pltpu.roll(line, cols - 1, 0))
    return left, right


def air_line(h, before, after):
    left, right = set_columns(h, before, after)
    return jnp.concatenate([left, h, right], axis=1).astype(BF16)


def sea_line(h, before, after):
    half = h.shape[1] // 2
    left, _ = set_columns(h[:, half:], before[:, half:], after[:, half:])
    _, right = set_columns(h[:, :half], before[:, :half], after[:, :half])
    return jnp.concatenate([left, h, right], axis=1).astype(BF16)


def air_product(block, kernel):
    return dot(block, kernel.reshape(-1, kernel.shape[-1]))


def sea_product(block, kernel):
    width = kernel.shape[-1]
    flat = kernel.reshape(-1, width)
    return jnp.concatenate(
        [dot(block[:, : 3 * width], flat), dot(block[:, width : 4 * width], flat)], axis=1
    )


def each_component(run, air_ref, sea_ref):
    ocean = on_ocean()

    @pl.when(jnp.logical_not(ocean))
    def _():
        run(air_ref, air_line, air_product, False)

    @pl.when(ocean)
    def _():
        run(sea_ref, sea_line, sea_product, True)


def halo_conv_kernel(
    layer, x_ref, top_ref, bottom_ref, left_ref, right_ref, air_ref, sea_ref, sum_ref, lined
):
    rows, cols, width = x_ref.shape

    def run(kernels_ref, make_line, product, masked):
        wide = (2 if masked else 3) * width
        before_all = silu(left_ref[...])
        after_all = silu(right_ref[...])

        def put(r):
            line = top_ref[...] if r == 0 else bottom_ref[...] if r == rows + 1 else x_ref[r - 1]
            lined[r, :, 0:wide] = make_line(
                silu(line.astype(F32)), before_all[r : r + 1], after_all[r : r + 1]
            )

        put(0)
        put(1)
        for r0 in range(0, rows, GROUP):
            for k in range(GROUP):
                put(r0 + k + 2)
            total = x_ref[r0 : r0 + GROUP].astype(F32).reshape(GROUP * cols, width)
            for d in range(3):
                block = lined[r0 + d : r0 + d + GROUP, :, 0:wide].reshape(GROUP * cols, wide)
                total = total + product(block, kernels_ref[layer, d])
            sum_ref[r0 : r0 + GROUP] = total.reshape(GROUP, cols, width)

    each_component(run, air_ref, sea_ref)


def inside_conv_kernel(
    layer, begin, end, *refs
):
    if begin:
        refs = refs[1:]
    x_ref, water_ref, air_ref, sea_ref, out_hbm, line_ref, sides_ref, token_ref = refs[:8]
    lined, out, wide_water, turned, sems = refs[8:]
    rows, cols, width = x_ref.shape
    half = width // 2
    token_ref[...] = jnp.zeros_like(token_ref)

    def write(g):
        at = g * GROUP
        return pltpu.make_async_copy(
            out.at[pl.ds(at, GROUP)], out_hbm.at[pl.ds(begin + at, GROUP)], sems.at[g]
        )

    def run(kernels_ref, make_line, product, masked):
        wide = (2 if masked else 3) * width
        none = jnp.zeros((1, width), F32)

        def put(r):
            if 0 <= r < rows:
                line = make_line(silu(x_ref[r].astype(F32)), none, none)
            else:
                line = jnp.zeros((cols, wide), BF16)
            lined[r - begin + 1, :, 0:wide] = line

        if masked:
            fill_water(water_ref, wide_water, turned)
        put(begin - 1)
        put(begin)
        for r0 in range(begin, end, GROUP):
            for k in range(GROUP):
                put(r0 + k + 1)
            total = x_ref[r0 : r0 + GROUP].astype(F32).reshape(GROUP * cols, width)
            for d in range(3):
                at = r0 - begin + d
                block = lined[at : at + GROUP, :, 0:wide].reshape(GROUP * cols, wide)
                total = total + product(block, kernels_ref[layer, d])
            total = total.reshape(GROUP, cols, width)
            for k in range(GROUP):
                r = r0 + k
                line = total[k]
                if r == 0 or r == rows - 1:
                    line_ref[...] = line
                sides_ref[0, r - begin] = line[:BLOCK_COLS]
                sides_ref[1, r - begin] = line[cols - BLOCK_COLS :]
                if masked:
                    line = line * water_of_row(turned, rows, r, half, 0, cols)
                out[r - begin] = line.astype(BF16)
            write((r0 - begin) // GROUP).start()

    each_component(run, air_ref, sea_ref)
    for g in range((end - begin) // GROUP):
        write(g).wait()


def conv_cost(state, rows):
    cells = rows * state.shape[1]
    width = state.shape[2]
    return pl.CostEstimate(
        flops=2 * 9 * cells * width * width,
        bytes_accessed=cells * width * 6,
        transcendentals=cells * width,
    )


def conv_with_halo(layer, state, halo, air_kernels, sea_kernels):
    rows, cols, width = state.shape
    return pl.pallas_call(
        functools.partial(halo_conv_kernel, layer),
        out_shape=jax.ShapeDtypeStruct(state.shape, F32),
        in_specs=[VMEM] * 7,
        out_specs=VMEM,
        scratch_shapes=[pltpu.VMEM((rows + 2, cols, 3 * width), BF16)],
        compiler_params=params(),
        cost_estimate=conv_cost(state, rows),
        name="conv_halo",
    )(state, *halo, air_kernels, sea_kernels)


def conv_inside(layer, part, state, water, air_kernels, sea_kernels, out=None):
    rows, cols, width = state.shape
    count = rows // 2
    begin = part * count
    before = [] if out is None else [out]
    return pl.pallas_call(
        functools.partial(inside_conv_kernel, layer, begin, begin + count),
        out_shape=(
            jax.ShapeDtypeStruct(state.shape, BF16),
            jax.ShapeDtypeStruct((cols, width), F32),
            jax.ShapeDtypeStruct((2, count, BLOCK_COLS, width), F32),
            jax.ShapeDtypeStruct((8, 128), F32),
        ),
        in_specs=[HBM] * len(before) + [VMEM] * 4,
        out_specs=(HBM, VMEM, VMEM, VMEM),
        scratch_shapes=[
            pltpu.VMEM((count + 2, cols, 3 * width), BF16),
            pltpu.VMEM((count, cols, width), BF16),
        ]
        + water_scratch(cols)
        + [pltpu.SemaphoreType.DMA((count // GROUP,))],
        input_output_aliases={0: 0} if before else {},
        compiler_params=params(),
        cost_estimate=conv_cost(state, count),
        name="conv_inside",
    )(*before, state, water, air_kernels, sea_kernels)


def edge_kernel(
    layer, out_in_hbm, first_ref, last_ref, upper_ref, lower_ref, top_ref, bottom_ref, left_ref, right_ref,
    water_ref, air_ref, sea_ref, out_hbm, line_out, side_out, wide_water, turned, sems,
):
    del out_in_hbm
    rows = upper_ref.shape[1] + lower_ref.shape[1]
    cols, width = first_ref.shape
    half = width // 2
    inner = pl.ds(1, rows - 2)
    writes = [
        pltpu.make_async_copy(line_out.at[0], out_hbm.at[0], sems.at[0]),
        pltpu.make_async_copy(line_out.at[1], out_hbm.at[rows - 1], sems.at[1]),
        pltpu.make_async_copy(side_out.at[0], out_hbm.at[inner, pl.ds(0, BLOCK_COLS)], sems.at[2]),
        pltpu.make_async_copy(
            side_out.at[1], out_hbm.at[inner, pl.ds(cols - BLOCK_COLS, BLOCK_COLS)], sems.at[3]
        ),
    ]

    def run(kernels_ref, make_line, product, masked):
        none = jnp.zeros((1, width), F32)
        before = silu(left_ref[...])
        after = silu(right_ref[...])
        if masked:
            before, after = before[:, half:], after[:, :half]
            fill_water(water_ref, wide_water, turned)
        size = before.shape[1]
        west = jnp.zeros((rows, size), F32)
        east = jnp.zeros((rows, size), F32)
        for d in range(3):
            west = west + dot(before[d : d + rows].astype(BF16), kernels_ref[layer, d, 0])
            east = east + dot(after[d : d + rows].astype(BF16), kernels_ref[layer, d, 2])
        if masked:
            blank = jnp.zeros((rows, half), F32)
            west = jnp.concatenate([west, blank], axis=1)
            east = jnp.concatenate([blank, east], axis=1)

        def finish(value, r, start, size):
            if masked:
                value = value * water_of_row(turned, rows, r, half, start, size)
            return value.astype(BF16)

        at = iota((BLOCK_COLS, width), 0)
        for r in range(1, rows - 1):
            sides, k = (upper_ref, r) if r < rows // 2 else (lower_ref, r - rows // 2)
            total = sides[0, k] + jnp.where(at == 0, west[r : r + 1], 0.0)
            side_out[0, r - 1] = finish(total, r, 0, BLOCK_COLS)
            total = sides[1, k] + jnp.where(at == BLOCK_COLS - 1, east[r : r + 1], 0.0)
            side_out[1, r - 1] = finish(total, r, cols - BLOCK_COLS, BLOCK_COLS)
        writes[2].start()
        writes[3].start()
        at = iota((cols, width), 0)
        for k, (partial, line, d) in enumerate(((first_ref, top_ref, 0), (last_ref, bottom_ref, 2))):
            r = 0 if k == 0 else rows - 1
            lined = make_line(silu(line[...].astype(F32)), none, none)
            total = partial[...] + product(lined, kernels_ref[layer, d])
            total = total + jnp.where(at == 0, west[r : r + 1], 0.0)
            total = total + jnp.where(at == cols - 1, east[r : r + 1], 0.0)
            line_out[k] = finish(total, r, 0, cols)
            writes[k].start()

    each_component(run, air_ref, sea_ref)
    for copy in writes:
        copy.wait()


def fix_edges(layer, out, first, last, upper, lower, halo, water, air_kernels, sea_kernels):
    rows, cols, width = out.shape
    return pl.pallas_call(
        functools.partial(edge_kernel, layer),
        out_shape=jax.ShapeDtypeStruct(out.shape, BF16),
        in_specs=[HBM] + [VMEM] * 11,
        out_specs=HBM,
        scratch_shapes=[
            pltpu.VMEM((2, cols, width), BF16),
            pltpu.VMEM((2, rows - 2, BLOCK_COLS, width), BF16),
        ]
        + water_scratch(cols)
        + [pltpu.SemaphoreType.DMA((4,))],
        input_output_aliases={0: 0},
        compiler_params=params(),
        name="fix_edges",
    )(out, first, last, upper, lower, *halo, water, air_kernels, sea_kernels)


def update_kernel(
    labels_ref, first_hbm, second_hbm, sum_ref, water_ref, coupling_ref,
    new_ref, top_ref, bottom_ref, left_ref, right_ref,
    total, arrived, wide_water, turned, sems,
):
    rows, cols, width = new_ref.shape
    half = width // 2
    slots = first_hbm.shape[0]
    ocean = on_ocean()
    quarter = rows // 4
    halves = (first_hbm, second_hbm)

    def copy_of(h, s):
        return pltpu.make_async_copy(halves[h].at[s], arrived.at[h, s], sems.at[h, s])

    def each_slot(act):
        def one(s, _):
            label = labels_ref[s]

            @pl.when(label >= 0)
            def _():
                act(s, label)

            return 0

        lax.fori_loop(0, slots, one, 0)

    def fetch(s, label):
        copy_of(0, s).start()
        copy_of(1, s).start()

    each_slot(fetch)

    def store(r, line):
        low = line.astype(BF16)
        new_ref[r] = low
        put_rim((top_ref, bottom_ref, left_ref, right_ref), r, rows, low)

    @pl.when(jnp.logical_not(ocean))
    def _():
        total[:, :, 0:half] = jnp.zeros((rows, cols, half), F32)
        across = cols // BLOCK_COLS

        def add(s, label):
            r0 = (label // across) * BLOCK_ROWS
            c0 = pl.multiple_of((label % across) * BLOCK_COLS, BLOCK_COLS)
            for h in range(2):
                copy_of(h, s).wait()
                value = arrived[h, s].astype(F32).reshape(HALF_ROWS, BLOCK_COLS, half)
                total[pl.ds(r0 + h * HALF_ROWS, HALF_ROWS), pl.ds(c0, BLOCK_COLS), 0:half] += value

        each_slot(add)
        for k in range(4):
            r0 = k * quarter
            block = total[r0 : r0 + quarter, :, 0:half].astype(BF16).reshape(quarter * cols, half)
            force = dot(block, coupling_ref[...]).reshape(quarter, cols, width)
            for q in range(quarter):
                store(r0 + q, sum_ref[r0 + q] + force[q])

    @pl.when(ocean)
    def _():
        total[...] = jnp.zeros_like(total)
        fill_water(water_ref, wide_water, turned)
        wide = BLOCK_COLS // 2
        across = cols // wide

        def add(s, label):
            r0 = (label // across) * BLOCK_ROWS
            c0 = pl.multiple_of((label % across) * wide, wide)
            for h in range(2):
                copy_of(h, s).wait()
                value = arrived[h, s].astype(F32).reshape(2, HALF_ROWS, wide, half)
                for p in range(2):
                    total[
                        pl.ds(r0 + h * HALF_ROWS, HALF_ROWS), pl.ds(c0, wide), p * half : (p + 1) * half
                    ] += value[p]

        each_slot(add)
        for r in range(rows):
            store(r, (sum_ref[r] + total[r]) * water_of_row(turned, rows, r, half, 0, cols))


def update(labels, first, second, summed, water, coupling_matrix):
    rows, cols, width = summed.shape
    return pl.pallas_call(
        update_kernel,
        out_shape=(jax.ShapeDtypeStruct((rows, cols, width), BF16),) + rim_shapes(rows, cols, width),
        in_specs=[SMEM, HBM, HBM, VMEM, VMEM, VMEM],
        out_specs=(VMEM,) * 5,
        scratch_shapes=[
            pltpu.VMEM((rows, cols, width), F32),
            pltpu.VMEM((2,) + first.shape, BF16),
        ]
        + water_scratch(cols)
        + [pltpu.SemaphoreType.DMA((2, first.shape[0]))],
        compiler_params=params(),
        name="update",
    )(labels, first, second, summed, water, coupling_matrix)


def exchange(value, axis, bit):
    return lax.ppermute(value, axis, [(i, i ^ bit) for i in range(lax.axis_size(axis))])


def across_groups(value):
    return exchange(value, "grp", 1)


def to_owners(value):
    return lax.all_to_all(value, ("lat", "lon"), split_axis=0, concat_axis=0, tiled=True)


def all_lists(lists):
    held = across_groups(lists)[None]
    for axis in ("lon", "lat"):
        bit = 1
        while bit < lax.axis_size(axis):
            held = jnp.concatenate([held, exchange(held, axis, bit)], axis=0)
            bit *= 2
    return held


def rows_beside(top, bottom):
    lats = lax.axis_size("lat")
    above = lax.ppermute(bottom, "lat", [(i, i + 1) for i in range(lats - 1)])
    below = lax.ppermute(top, "lat", [(i + 1, i) for i in range(lats - 1)])
    return above, below


def columns_beside(west, east):
    lons = lax.axis_size("lon")
    before = lax.ppermute(east, "lon", [(i, (i + 1) % lons) for i in range(lons)])
    after = lax.ppermute(west, "lon", [((i + 1) % lons, i) for i in range(lons)])
    return before, after


def body(
    state,
    intersection_lists,
    intersection_matrices,
    water,
    air_kernels,
    sea_kernels,
    flux_projection,
    coupling_matrix,
):
    current = state[0]
    tiles = lax.axis_size("lat") * lax.axis_size("lon")
    entries = intersection_lists.shape[-1]
    lists = intersection_lists.reshape(3, entries)
    matrices = intersection_matrices.reshape(entries, BLOCK, BLOCK)

    first, second, lists, top, bottom, left, right = payloads(
        lists, current, matrices, water, flux_projection, tiles
    )
    first = across_groups(first)
    second = to_owners(second)
    above, below = rows_beside(top, bottom)
    first, labels, west, east = pack(all_lists(lists), first, above, below, left, right)
    second = across_groups(second)
    first = to_owners(first)
    before, after = columns_beside(west, east)
    summed = conv_with_halo(0, current, (above, below, before, after), air_kernels, sea_kernels)
    current, top, bottom, left, right = update(labels, first, second, summed, water, coupling_matrix)

    above, below = rows_beside(top, bottom)
    out, first, upper, token = conv_inside(1, 0, current, water, air_kernels, sea_kernels)
    corner = token[0, 0]
    west = jnp.concatenate([above[:1].astype(F32), left, below[:1].astype(F32)], axis=0) + corner
    east = jnp.concatenate([above[-1:].astype(F32), right, below[-1:].astype(F32)], axis=0) + corner
    before, after = columns_beside(west, east)
    out, last, lower, _ = conv_inside(1, 1, current, water, air_kernels, sea_kernels, out)
    out = fix_edges(
        1, out, first, last, upper, lower, (above, below, before, after), water, air_kernels, sea_kernels
    )
    return out[None]


def solution(mesh):
    placed = (
        P("grp", "lat", "lon", None),
        P("grp", "lat", "lon", None, None),
        P("grp", "lat", "lon", None, None, None),
        P("lat", "lon"),
        P(),
        P(),
        P(),
        P(),
    )
    return jax.shard_map(
        body, mesh=mesh, in_specs=placed, out_specs=P("grp", "lat", "lon", None), check_vma=False
    )
```

```python
import functools

import jax
import jax.numpy as jnp
from jax import lax
from jax.experimental import pallas as pl
from jax.experimental.pallas import tpu as pltpu
from jax.sharding import PartitionSpec as P

BLOCK_ROWS = 8
BLOCK_COLS = 16
BLOCK = BLOCK_ROWS * BLOCK_COLS
SLOTS = 2
FIRST = (1, 2, 3, 4, 5, 6)
SECOND = (0, 7)
FIRST_CELLS = len(FIRST) * BLOCK_COLS
SECOND_CELLS = len(SECOND) * BLOCK_COLS
LABEL_ROWS = 16
LANES = 128
VMEM_BYTES = 62 * 2**20
LATE_BYTES = 36 * 2**20
UPDATE_BYTES = 36 * 2**20

F32 = jnp.float32
BF16 = jnp.bfloat16

VMEM = pl.BlockSpec(memory_space=pltpu.VMEM)
SMEM = pl.BlockSpec(memory_space=pltpu.SMEM)
HBM = pl.BlockSpec(memory_space=pltpu.HBM)


def silu(v):
    h = 0.5 * v
    return h + h * jnp.tanh(h)


def iota(shape, dim):
    return lax.broadcasted_iota(jnp.int32, shape, dim)


def dot(a, b):
    return jnp.dot(a, b, preferred_element_type=F32)


def params(limit=VMEM_BYTES):
    return pltpu.CompilerParams(vmem_limit_bytes=limit)


def on_ocean():
    return lax.axis_index("grp") == 1


def fill_water(water_ref, wide_ref, turned_ref):
    rows, longitudes = water_ref.shape
    wide_ref[:, 0:rows] = water_ref[...].astype(F32).T
    for p in range(2):
        turned_ref[:, p * rows : (p + 1) * rows] = wide_ref[pl.ds(p, longitudes // 2, stride=2), :][:, 0:rows]


def water_scratch(cols):
    return [pltpu.VMEM((2 * cols, 128), F32), pltpu.VMEM((cols, 128), F32)]


def water_of_row(turned_ref, rows, r, width, start, size):
    parts = [
        jnp.broadcast_to(turned_ref[start : start + size, p * rows + r : p * rows + r + 1], (size, width))
        for p in range(2)
    ]
    return jnp.concatenate(parts, axis=1)


def rim_shapes(rows, cols, width):
    line = jax.ShapeDtypeStruct((cols, width), BF16)
    side = jax.ShapeDtypeStruct((rows, width), F32)
    return (line, line, side, side)


def put_rim(rim, r, rows, line):
    top_ref, bottom_ref, left_ref, right_ref = rim
    cols = line.shape[0]
    exact = line.astype(F32)
    left_ref[r : r + 1] = exact[0:1]
    right_ref[r : r + 1] = exact[cols - 1 : cols]
    if r == 0:
        top_ref[...] = line
    if r == rows - 1:
        bottom_ref[...] = line


def payload_kernel(
    lists_in, state_hbm, matrices_hbm, water_ref, flux_hbm,
    first_ref, second_ref, lists_out, top_ref, bottom_ref, left_ref, right_ref,
    state_ref, matrices_ref, flux_ref, flux, surface, wide_water, turned, count, sems,
):
    rows, cols, width = state_ref.shape
    half = width // 2
    entries = matrices_ref.shape[0]
    tiles = second_ref.shape[0]
    ocean = on_ocean()
    pieces = 4
    step = rows // pieces
    flux_copy = pltpu.make_async_copy(flux_hbm, flux_ref, sems.at[pieces])
    matrices_copy = pltpu.make_async_copy(matrices_hbm, matrices_ref, sems.at[pieces + 1])
    state_copies = [
        pltpu.make_async_copy(state_hbm.at[pl.ds(k * step, step)], state_ref.at[pl.ds(k * step, step)], sems.at[k])
        for k in range(pieces)
    ]
    lists_ref = lists_in.at[0, 0, 0]
    flux_copy.start()
    for copy in state_copies:
        copy.start()
    matrices_copy.start()

    def clear(t, _):
        count[t] = 0
        return 0

    lax.fori_loop(0, tiles, clear, 0)

    def keep(e, _):
        for k in range(3):
            lists_out[k, e] = lists_ref[k, e]
        return 0

    lax.fori_loop(0, entries, keep, 0)
    second_ref[:, SLOTS * SECOND_CELLS :, :] = jnp.full((tiles, LABEL_ROWS, half), -1.0, BF16)
    i = iota((BLOCK, BLOCK), 0)
    j = iota((BLOCK, BLOCK), 1)

    def put(e, payload, cut):
        owner = lists_ref[0, e]
        rank = count[owner]
        count[owner] = rank + 1
        first_ref[e], second = cut(payload)
        at = pl.multiple_of(rank * SECOND_CELLS, BLOCK_COLS)
        second_ref[owner, pl.ds(at, SECOND_CELLS), :] = second
        label = jnp.full((LABEL_ROWS, LANES), lists_ref[2, e], jnp.int32).astype(F32).astype(BF16)
        second_ref[owner, SLOTS * SECOND_CELLS :, pl.ds(pl.multiple_of(rank * LANES, LANES), LANES)] = label

    flux_copy.wait()

    @pl.when(jnp.logical_not(ocean))
    def _():
        wide = BLOCK_COLS // 2
        c = i % wide
        p1, r1 = i // (FIRST_CELLS // 2), FIRST[0] + i % (FIRST_CELLS // 2) // wide
        k = i - FIRST_CELLS
        q = k % (SECOND_CELLS // 2) // wide
        p2, r2 = k // (SECOND_CELLS // 2), jnp.where(q == 0, 0, q + FIRST[-1])
        p, r = jnp.where(k < 0, p1, p2), jnp.where(k < 0, r1, r2)
        turn = (j == r * BLOCK_COLS + 2 * c + p).astype(BF16)
        for k in range(pieces):
            state_copies[k].wait()
            block = state_ref[k * step : (k + 1) * step].reshape(step * cols, width)
            flux[k * step : (k + 1) * step] = (
                dot(block, flux_ref[...]).astype(BF16).reshape(step, cols, half)
            )
        matrices_copy.wait()
        across = cols // BLOCK_COLS

        def entry(e, _):
            source = lists_ref[1, e]
            r0 = (source // across) * BLOCK_ROWS
            c0 = pl.multiple_of((source % across) * BLOCK_COLS, BLOCK_COLS)
            chosen = flux[pl.ds(r0, BLOCK_ROWS), pl.ds(c0, BLOCK_COLS), :].reshape(BLOCK, half)
            weight = dot(turn, matrices_ref[e]).astype(BF16)
            put(e, dot(weight, chosen).astype(BF16), lambda v: (v[:FIRST_CELLS], v[FIRST_CELLS:]))
            return 0

        lax.fori_loop(0, entries, entry, 0, unroll=8)

    @pl.when(ocean)
    def _():
        p, r, c = j // 64, (j // 8) % 8, j % 8
        turn = (i == r * BLOCK_COLS + 2 * c + p).astype(BF16)
        fill_water(water_ref, wide_water, turned)
        for k in range(pieces):
            state_copies[k].wait()
            for r0 in range(k * step, (k + 1) * step):
                surface[r0] = state_ref[r0].astype(F32) * water_of_row(turned, rows, r0, half, 0, cols)
        matrices_copy.wait()
        wide = BLOCK_COLS // 2
        across = cols // wide

        def entry(e, _):
            source = lists_ref[1, e]
            r0 = (source // across) * BLOCK_ROWS
            c0 = pl.multiple_of((source % across) * wide, wide)
            block = surface[pl.ds(r0, BLOCK_ROWS), pl.ds(c0, wide), :]
            chosen = jnp.concatenate(
                [block[:, :, q * half : (q + 1) * half].reshape(BLOCK // 2, half) for q in range(2)], axis=0
            ).astype(BF16)
            weight = dot(matrices_ref[e], turn).astype(BF16)
            low, high = BLOCK_COLS, BLOCK_COLS + FIRST_CELLS
            put(
                e,
                dot(weight, chosen).astype(BF16),
                lambda v: (v[low:high], jnp.concatenate([v[:low], v[high:]], axis=0)),
            )
            return 0

        lax.fori_loop(0, entries, entry, 0, unroll=8)

    for r in range(rows):
        put_rim((top_ref, bottom_ref, left_ref, right_ref), r, rows, state_ref[r])


def payloads(lists, state, matrices, water, flux_projection, tiles):
    rows, cols, width = state.shape
    half = width // 2
    entries = lists.shape[-1]
    return pl.pallas_call(
        payload_kernel,
        out_shape=(
            jax.ShapeDtypeStruct((entries, FIRST_CELLS, half), BF16),
            jax.ShapeDtypeStruct((tiles, SLOTS * SECOND_CELLS + LABEL_ROWS, half), BF16),
            jax.ShapeDtypeStruct((3, entries), jnp.int32),
        )
        + rim_shapes(rows, cols, width),
        in_specs=[SMEM, HBM, HBM, VMEM, HBM],
        out_specs=(VMEM, VMEM, SMEM) + (VMEM,) * 4,
        scratch_shapes=[
            pltpu.VMEM(state.shape, BF16),
            pltpu.VMEM(matrices.shape, BF16),
            pltpu.VMEM(flux_projection.shape, BF16),
            pltpu.VMEM((rows, cols, half), BF16),
            pltpu.VMEM((rows, cols, width), F32),
        ]
        + water_scratch(cols)
        + [
            pltpu.SMEM((tiles,), jnp.int32),
            pltpu.SemaphoreType.DMA((6,)),
        ],
        compiler_params=params(),
        name="payload",
    )(lists, state, matrices, water, flux_projection)


def pack_kernel(
    lists_ref, dense_ref, above_ref, below_ref, left_ref, right_ref, token_ref, slots_ref, west_ref, east_ref, count
):
    entries = lists_ref.shape[1]
    tiles = slots_ref.shape[0]

    def clear(t, _):
        count[t] = 0
        return 0

    lax.fori_loop(0, tiles, clear, 0)

    def place(e, _):
        owner = lists_ref[0, e]
        rank = count[owner]
        count[owner] = rank + 1
        at = pl.multiple_of(rank * FIRST_CELLS, BLOCK_COLS)
        slots_ref[owner, pl.ds(at, FIRST_CELLS), :] = dense_ref[e]
        return 0

    lax.fori_loop(0, entries, place, 0, unroll=4)
    del token_ref
    put_sides(above_ref, below_ref, left_ref, right_ref, west_ref, east_ref)


def pack(tiles, lists, dense, above, below, left, right, token):
    rows, width = left.shape
    side = jax.ShapeDtypeStruct((rows + 2, width), F32)
    return pl.pallas_call(
        pack_kernel,
        out_shape=(jax.ShapeDtypeStruct((tiles, SLOTS * FIRST_CELLS, dense.shape[2]), BF16), side, side),
        in_specs=[SMEM] + [VMEM] * 5 + [HBM],
        out_specs=(VMEM,) * 3,
        scratch_shapes=[pltpu.SMEM((tiles,), jnp.int32)],
        compiler_params=params(),
        name="pack",
    )(lists, dense, above, below, left, right, token)


def put_sides(above_ref, below_ref, left_ref, right_ref, west_ref, east_ref):
    rows = left_ref.shape[0]
    cols = above_ref.shape[0]
    for ref, side, at in ((west_ref, left_ref, 0), (east_ref, right_ref, cols - 1)):
        ref[0:1] = above_ref[at : at + 1].astype(F32)
        ref[1 : rows + 1] = side[...]
        ref[rows + 1 : rows + 2] = below_ref[at : at + 1].astype(F32)


def slot_labels(second):
    return second[:, SLOTS * SECOND_CELLS, ::LANES][:, :SLOTS].astype(jnp.int32).reshape(-1)


GROUP = 4


TILE = 8


def set_columns(line, before, after):
    cols = line.shape[0]
    left, right = pltpu.roll(line, 1, 0), pltpu.roll(line, cols - 1, 0)
    at = iota((TILE, line.shape[1]), 0)
    head = jnp.where(at == 0, before, left[:TILE])
    tail = jnp.where(at == TILE - 1, after, right[cols - TILE :])
    left = jnp.concatenate([head, left[TILE:]], axis=0)
    right = jnp.concatenate([right[: cols - TILE], tail], axis=0)
    return left, right


def air_line(h, before, after):
    left, right = set_columns(h, before, after)
    return jnp.concatenate([left, h, right], axis=1).astype(BF16)


def sea_line(h, before, after):
    half = h.shape[1] // 2
    left, _ = set_columns(h[:, half:], before[:, half:], after[:, half:])
    _, right = set_columns(h[:, :half], before[:, :half], after[:, :half])
    return jnp.concatenate([left, h, right], axis=1).astype(BF16)


def air_product(block, kernel):
    return dot(block, kernel.reshape(-1, kernel.shape[-1]))


def sea_product(block, kernel):
    width = kernel.shape[-1]
    flat = kernel.reshape(-1, width)
    return jnp.concatenate(
        [dot(block[:, : 3 * width], flat), dot(block[:, width : 4 * width], flat)], axis=1
    )


def each_component(run, air, sea):
    ocean = on_ocean()

    @pl.when(jnp.logical_not(ocean))
    def _():
        run(air, air_line, air_product, False)

    @pl.when(ocean)
    def _():
        run(sea, sea_line, sea_product, True)


def held_weights(air_kernels):
    return [pltpu.VMEM(air_kernels.shape[1:], BF16), pltpu.SemaphoreType.DMA((3, 3))]


def fetch_weights(layer, kernels_hbm, held, sems, wanted):
    width = kernels_hbm.shape[-1]
    copies = {
        (d, c): pltpu.make_async_copy(
            kernels_hbm.at[layer, d, c], held.at[d, c, pl.ds(0, width), pl.ds(0, width)], sems.at[d, c]
        )
        for d, c in wanted
    }
    for copy in copies.values():
        copy.start()
    return copies


def inside_conv_kernel(layer, begin, end, keep, *refs):
    x_hbm, _, air_hbm, sea_hbm, out_hbm, last_out = refs[:6]
    x_ref, lined, out, held, weight_sems, x_sems, sems = refs[6:13]
    rows, cols, width = x_hbm.shape
    low, high = max(begin - 1, 0), min(end + 1, rows)
    groups = (end - begin) // GROUP
    early = begin + GROUP + 1
    spans = [(low, early), (early, high)]
    every = [(d, c) for d in range(3) for c in range(3)]
    kept_write = None
    if keep:
        kept, kept_sems, kept_sem = refs[13:]
        kept_write = pltpu.make_async_copy(kept, last_out, kept_sem)
    else:
        last_out[...] = jnp.zeros_like(last_out)

    def read(k):
        at = pl.ds(spans[k][0], spans[k][1] - spans[k][0])
        return pltpu.make_async_copy(x_hbm.at[at], x_ref.at[at], x_sems.at[k])

    def write(g):
        at = g * GROUP
        return pltpu.make_async_copy(
            out.at[pl.ds(at, GROUP)], out_hbm.at[pl.ds(begin + at, GROUP)], sems.at[g]
        )

    def run(kernels_hbm, make_line, product, masked):
        wide = (2 if masked else 3) * width
        size = width // 2 if masked else width
        none = jnp.zeros((1, width), F32)
        read(0).start()
        weights = fetch_weights(layer, kernels_hbm, held, weight_sems, every)
        read(1).start()
        later = fetch_weights(layer + 1, kernels_hbm, kept, kept_sems, every) if keep else {}

        def put(r):
            if 0 <= r < rows:
                line = make_line(silu(x_ref[r].astype(F32)), none, none)
            else:
                line = jnp.zeros((cols, wide), BF16)
            lined[r - begin + 1, :, 0:wide] = line

        read(0).wait()
        for r in range(begin - 1, early):
            put(r)
        for copy in weights.values():
            copy.wait()
        read(1).wait()
        for g in range(groups):
            r0 = begin + g * GROUP
            total = x_ref[r0 : r0 + GROUP].astype(F32).reshape(GROUP * cols, width)
            for d in range(3):
                at = r0 - begin + d
                block = lined[at : at + GROUP, :, 0:wide].reshape(GROUP * cols, wide)
                total = total + product(block, held[d, :, 0:size, 0:size])
            if g + 1 < groups:
                for r in range(r0 + GROUP + 1, r0 + 2 * GROUP + 1):
                    put(r)
            out[r0 - begin : r0 - begin + GROUP] = total.reshape(GROUP, cols, width)
            write(g).start()
            if keep and g == 0:
                for copy in later.values():
                    copy.wait()
                kept_write.start()

    each_component(run, air_hbm, sea_hbm)
    for g in range(groups):
        write(g).wait()
    if keep:
        kept_write.wait()


def last_conv_kernel(
    x_ref, above_ref, below_ref, water_ref, held, out_hbm, sides_ref, lined, out, wide_water, turned, sems
):
    rows, cols, width = x_ref.shape
    half = width // 2
    groups = rows // GROUP

    def write(g):
        at = pl.ds(g * GROUP, GROUP)
        return pltpu.make_async_copy(out.at[at], out_hbm.at[at], sems.at[g])

    def run(_, make_line, product, masked):
        wide = (2 if masked else 3) * width
        size = half if masked else width
        none = jnp.zeros((1, width), F32)

        def put(r):
            line = above_ref[...] if r < 0 else below_ref[...] if r == rows else x_ref[r]
            lined[r + 1, :, 0:wide] = make_line(silu(line.astype(F32)), none, none)

        if masked:
            fill_water(water_ref, wide_water, turned)
        for r in range(-1, GROUP + 1):
            put(r)
        for g in range(groups):
            r0 = g * GROUP
            total = x_ref[r0 : r0 + GROUP].astype(F32).reshape(GROUP * cols, width)
            for d in range(3):
                block = lined[r0 + d : r0 + d + GROUP, :, 0:wide].reshape(GROUP * cols, wide)
                total = total + product(block, held[d, :, 0:size, 0:size])
            if g + 1 < groups:
                for r in range(r0 + GROUP + 1, r0 + 2 * GROUP + 1):
                    put(r)
            total = total.reshape(GROUP, cols, width)
            for k in range(GROUP):
                r = r0 + k
                line = total[k]
                sides_ref[0, r] = line[:BLOCK_COLS]
                sides_ref[1, r] = line[cols - BLOCK_COLS :]
                if masked:
                    line = line * water_of_row(turned, rows, r, half, 0, cols)
                out[r] = line.astype(BF16)
            write(g).start()

    each_component(run, None, None)
    for g in range(groups):
        write(g).wait()


def last_conv(state, above, below, water, held):
    rows, cols, width = state.shape
    return pl.pallas_call(
        last_conv_kernel,
        out_shape=(
            jax.ShapeDtypeStruct(state.shape, BF16),
            jax.ShapeDtypeStruct((2, rows, BLOCK_COLS, width), F32),
        ),
        in_specs=[VMEM] * 5,
        out_specs=(HBM, VMEM),
        scratch_shapes=[
            pltpu.VMEM((rows + 2, cols, 3 * width), BF16),
            pltpu.VMEM((rows, cols, width), BF16),
        ]
        + water_scratch(cols)
        + [pltpu.SemaphoreType.DMA((rows // GROUP,))],
        compiler_params=params(LATE_BYTES),
        cost_estimate=conv_cost(state, rows),
        name="last_conv",
    )(state, above, below, water, held)


def conv_cost(state, rows):
    cells = rows * state.shape[1]
    width = state.shape[2]
    return pl.CostEstimate(
        flops=2 * 9 * cells * width * width,
        bytes_accessed=cells * width * 6 + 9 * width * width * 2,
        transcendentals=cells * width,
    )


def conv_inside(layer, begin, end, state, after, air_kernels, sea_kernels, keep):
    rows, cols, width = state.shape
    count = end - begin
    kernel_shape = air_kernels.shape[1:]
    scratch = [
        pltpu.VMEM(state.shape, BF16),
        pltpu.VMEM((count + 2, cols, 3 * width), BF16),
        pltpu.VMEM((count, cols, width), F32),
    ] + held_weights(air_kernels)
    scratch += [pltpu.SemaphoreType.DMA((2,)), pltpu.SemaphoreType.DMA((count // GROUP,))]
    if keep:
        scratch += held_weights(air_kernels) + [pltpu.SemaphoreType.DMA]
    return pl.pallas_call(
        functools.partial(inside_conv_kernel, layer, begin, end, keep),
        out_shape=(
            jax.ShapeDtypeStruct(state.shape, F32),
            jax.ShapeDtypeStruct(kernel_shape, BF16) if keep else jax.ShapeDtypeStruct((8, 128), F32),
        ),
        in_specs=[HBM] * 4,
        out_specs=(HBM, HBM if keep else VMEM),
        scratch_shapes=scratch,
        input_output_aliases={1: 0} if keep else {},
        compiler_params=params(),
        cost_estimate=conv_cost(state, count),
        name="conv_inside",
    )(state, after, air_kernels, sea_kernels)


EDGE_WEIGHTS = [(0, 0), (1, 0), (2, 0), (0, 2), (1, 2), (2, 2), (0, 1), (2, 1)]


def halo_columns(rows, left_ref, right_ref, weights, held, masked):
    before = silu(left_ref[...])
    after = silu(right_ref[...])
    half = before.shape[1] // 2
    if masked:
        before, after = before[:, half:], after[:, :half]
    west = jnp.zeros((rows, before.shape[1]), F32)
    east = jnp.zeros((rows, before.shape[1]), F32)
    size = before.shape[1]
    for d in range(3):
        if weights:
            weights[d, 0].wait()
        west = west + dot(before[d : d + rows].astype(BF16), held[d, 0, 0:size, 0:size])
    for d in range(3):
        if weights:
            weights[d, 2].wait()
        east = east + dot(after[d : d + rows].astype(BF16), held[d, 2, 0:size, 0:size])
    if masked:
        blank = jnp.zeros((rows, half), F32)
        west = jnp.concatenate([west, blank], axis=1)
        east = jnp.concatenate([blank, east], axis=1)
    return west, east


def side_kernel(
    out_in_hbm, sides_ref, left_ref, right_ref, water_ref, held, out_hbm, side_out, wide_water, turned, sems,
):
    del out_in_hbm
    rows, cols, width = out_hbm.shape
    half = width // 2
    writes = [
        pltpu.make_async_copy(side_out.at[k], out_hbm.at[:, pl.ds(start, BLOCK_COLS)], sems.at[k])
        for k, start in enumerate((0, cols - BLOCK_COLS))
    ]

    def run(_, make_line, product, masked):
        if masked:
            fill_water(water_ref, wide_water, turned)
        added = halo_columns(rows, left_ref, right_ref, None, held, masked)
        at = iota((BLOCK_COLS, width), 0)
        for k, (start, here) in enumerate(((0, 0), (cols - BLOCK_COLS, BLOCK_COLS - 1))):
            for r in range(rows):
                total = sides_ref[k, r] + jnp.where(at == here, added[k][r : r + 1], 0.0)
                if masked:
                    total = total * water_of_row(turned, rows, r, half, start, BLOCK_COLS)
                side_out[k, r] = total.astype(BF16)
            writes[k].start()

    each_component(run, None, None)
    for copy in writes:
        copy.wait()


def fix_sides(out, sides, beside, water, held):
    rows, cols, width = out.shape
    return pl.pallas_call(
        side_kernel,
        out_shape=jax.ShapeDtypeStruct(out.shape, BF16),
        in_specs=[HBM] + [VMEM] * 5,
        out_specs=HBM,
        scratch_shapes=[pltpu.VMEM((2, rows, BLOCK_COLS, width), BF16)]
        + water_scratch(cols)
        + [pltpu.SemaphoreType.DMA((2,))],
        input_output_aliases={0: 0},
        compiler_params=params(LATE_BYTES),
        name="fix_sides",
    )(out, sides, *beside, water, held)


def edge_copies(rows, cols, count, lines, sides, hbm, sems, inward):
    inner = pl.ds(1, rows - 2)
    pairs = [
        (lines.at[0], hbm.at[0]),
        (lines.at[1], hbm.at[rows - 1]),
        (sides.at[0], hbm.at[inner, pl.ds(0, count)]),
        (sides.at[1], hbm.at[inner, pl.ds(cols - count, count)]),
    ]
    return [
        pltpu.make_async_copy(*(pair[::-1] if inward else pair), sems.at[k]) for k, pair in enumerate(pairs)
    ]


SIDE = 8


def sum_edge_kernel(
    layer, sum_in_hbm, top_ref, bottom_ref, left_ref, right_ref, air_hbm, sea_hbm, sum_hbm,
    lines, sides, held, weight_sems, read_sems, sems,
):
    rows, cols, width = sum_hbm.shape
    reads = edge_copies(rows, cols, SIDE, lines, sides, sum_in_hbm, read_sems, True)
    writes = edge_copies(rows, cols, SIDE, lines, sides, sum_hbm, sems, False)
    for copy in reads:
        copy.start()

    def run(kernels_hbm, make_line, product, masked):
        size = width // 2 if masked else width
        weights = fetch_weights(layer, kernels_hbm, held, weight_sems, EDGE_WEIGHTS)
        none = jnp.zeros((1, width), F32)
        west, east = halo_columns(rows, left_ref, right_ref, weights, held, masked)
        for copy in reads:
            copy.wait()
        at = iota((SIDE, width), 0)
        for r in range(1, rows - 1):
            sides[0, r - 1] += jnp.where(at == 0, west[r : r + 1], 0.0)
            sides[1, r - 1] += jnp.where(at == SIDE - 1, east[r : r + 1], 0.0)
        at = iota((cols, width), 0)
        for k, (line, d) in enumerate(((top_ref, 0), (bottom_ref, 2))):
            r = 0 if k == 0 else rows - 1
            lined = make_line(silu(line[...].astype(F32)), none, none)
            weights[d, 1].wait()
            total = lines[k] + product(lined, held[d, :, 0:size, 0:size])
            total = total + jnp.where(at == 0, west[r : r + 1], 0.0)
            lines[k] = total + jnp.where(at == cols - 1, east[r : r + 1], 0.0)

    each_component(run, air_hbm, sea_hbm)
    for copy in writes:
        copy.start()
    for copy in writes:
        copy.wait()


def add_edges(layer, summed, halo, air_kernels, sea_kernels):
    rows, cols, width = summed.shape
    return pl.pallas_call(
        functools.partial(sum_edge_kernel, layer),
        out_shape=jax.ShapeDtypeStruct(summed.shape, F32),
        in_specs=[HBM] + [VMEM] * 4 + [HBM] * 2,
        out_specs=HBM,
        scratch_shapes=[
            pltpu.VMEM((2, cols, width), F32),
            pltpu.VMEM((2, rows - 2, SIDE, width), F32),
        ]
        + held_weights(air_kernels)
        + [pltpu.SemaphoreType.DMA((4,)), pltpu.SemaphoreType.DMA((4,))],
        input_output_aliases={0: 0},
        compiler_params=params(),
        name="add_edges",
    )(summed, *halo, air_kernels, sea_kernels)


def runs_of(block_rows, rows):
    runs = []
    for r in range(rows):
        if r % BLOCK_ROWS in block_rows:
            if runs and sum(runs[-1]) == r:
                runs[-1] = (runs[-1][0], runs[-1][1] + 1)
            else:
                runs.append((r, 1))
    return runs


def update_kernel(block_rows, last, *refs):
    if last:
        (labels_ref, message_hbm, sum_hbm, water_ref, coupling_hbm, early_new, above_ref, below_ref) = refs[:8]
        (early_left, early_right, new_ref, west_ref, east_ref) = refs[8:13]
        refs = refs[13:]
        left_ref, right_ref, refs = refs[0], refs[1], refs[2:]
    else:
        (labels_ref, message_hbm, sum_hbm, water_ref, coupling_hbm) = refs[:5]
        new_ref, top_ref, bottom_ref = refs[5:8]
        refs = refs[8:]
    (total, message, sum_ref, coupling_ref, wide_water, turned) = refs[:6]
    (message_sem, coupling_sem, sum_sems) = refs[6:]
    rows, cols, width = sum_ref.shape
    half = width // 2
    slots = message_hbm.shape[0] * SLOTS
    cells = len(block_rows) * BLOCK_COLS
    runs = runs_of(block_rows, rows)
    parts = [(start, count, block_rows.index(start)) for start, count in runs_of(block_rows, BLOCK_ROWS)]
    updated = [r for start, count in runs for r in range(start, start + count)]
    ocean = on_ocean()

    def run_copy(source, target, k, sems):
        at = pl.ds(*runs[k])
        return pltpu.make_async_copy(source.at[at], target.at[at], sems.at[k])

    message_copy = pltpu.make_async_copy(message_hbm, message, message_sem)
    coupling_copy = pltpu.make_async_copy(coupling_hbm, coupling_ref, coupling_sem)
    message_copy.start()
    for k in range(len(runs)):
        run_copy(sum_hbm, sum_ref, k, sum_sems).start()
    coupling_copy.start()
    if last:
        at = 0
        for start, count in runs_of([r for r in range(BLOCK_ROWS) if r not in block_rows], rows):
            new_ref[start : start + count] = early_new[at : at + count]
            at += count
        left_ref[...] = early_left[...]
        right_ref[...] = early_right[...]

    def clear(lanes):
        for start, count in runs:
            total[start : start + count, :, 0:lanes] = jnp.zeros((count, cols, lanes), F32)

    def each_slot(act):
        def one(s, _):
            label = labels_ref[s]

            @pl.when(label >= 0)
            def _():
                at = pl.multiple_of((s % SLOTS) * cells, BLOCK_COLS)
                act(message[s // SLOTS, pl.ds(at, cells), :].astype(F32), label)

            return 0

        lax.fori_loop(0, slots, one, 0)

    def store(r, line):
        low = line.astype(BF16)
        new_ref[r if last else updated.index(r)] = low
        if last:
            left_ref[r : r + 1] = low[:TILE].astype(F32)[:1]
            right_ref[r : r + 1] = low[cols - TILE :].astype(F32)[TILE - 1 :]
        elif r == 0:
            top_ref[...] = low
        elif r == rows - 1:
            bottom_ref[...] = low

    @pl.when(jnp.logical_not(ocean))
    def _():
        clear(half)
        across = cols // BLOCK_COLS

        def add(value, label):
            r0 = (label // across) * BLOCK_ROWS
            c0 = pl.multiple_of((label % across) * BLOCK_COLS, BLOCK_COLS)
            value = value.reshape(len(block_rows), BLOCK_COLS, half)
            for start, count, at in parts:
                total[pl.ds(r0 + start, count), pl.ds(c0, BLOCK_COLS), 0:half] += value[at : at + count]

        message_copy.wait()
        each_slot(add)
        coupling_copy.wait()
        for k, (start, count) in enumerate(runs):
            block = total[start : start + count, :, 0:half].astype(BF16).reshape(count * cols, half)
            force = dot(block, coupling_ref[...]).reshape(count, cols, width)
            run_copy(sum_hbm, sum_ref, k, sum_sems).wait()
            for q in range(count):
                store(start + q, sum_ref[start + q] + force[q])

    @pl.when(ocean)
    def _():
        clear(width)
        fill_water(water_ref, wide_water, turned)
        wide = BLOCK_COLS // 2
        across = cols // wide

        def add(value, label):
            r0 = (label // across) * BLOCK_ROWS
            c0 = pl.multiple_of((label % across) * wide, wide)
            value = value.reshape(2, len(block_rows), wide, half)
            for start, count, at in parts:
                for p in range(2):
                    lanes = slice(p * half, (p + 1) * half)
                    total[pl.ds(r0 + start, count), pl.ds(c0, wide), lanes] += value[p, at : at + count]

        message_copy.wait()
        each_slot(add)
        coupling_copy.wait()
        for k, (start, count) in enumerate(runs):
            run_copy(sum_hbm, sum_ref, k, sum_sems).wait()
            for r in range(start, start + count):
                store(r, (sum_ref[r] + total[r]) * water_of_row(turned, rows, r, half, 0, cols))

    if last:
        put_sides(above_ref, below_ref, left_ref, right_ref, west_ref, east_ref)


def update(block_rows, labels, message, summed, water, coupling_matrix, early=None):
    rows, cols, width = summed.shape
    last = early is not None
    side = jax.ShapeDtypeStruct((rows + 2, width), F32)
    runs = len(runs_of(block_rows, rows))
    count = rows if last else rows // BLOCK_ROWS * len(block_rows)
    kept = [pltpu.VMEM((rows, width), F32)] * 2 if last else []
    return pl.pallas_call(
        functools.partial(update_kernel, block_rows, last),
        out_shape=(jax.ShapeDtypeStruct((count, cols, width), BF16),)
        + ((side, side) if last else rim_shapes(rows, cols, width)[:2]),
        in_specs=[SMEM, HBM, HBM, VMEM, HBM] + ([VMEM] * 5 if last else []),
        out_specs=(VMEM,) * 3,
        scratch_shapes=kept
        + [
            pltpu.VMEM((rows, cols, width), F32),
            pltpu.VMEM(message.shape, BF16),
            pltpu.VMEM((rows, cols, width), F32),
            pltpu.VMEM(coupling_matrix.shape, BF16),
        ]
        + water_scratch(cols)
        + [
            pltpu.SemaphoreType.DMA,
            pltpu.SemaphoreType.DMA,
            pltpu.SemaphoreType.DMA((runs,)),
        ],
        compiler_params=params(UPDATE_BYTES if last else VMEM_BYTES),
        name="update",
    )(labels, message, summed, water, coupling_matrix, *(early or ()))


def early_sides_kernel(new_ref, left_ref, right_ref):
    rows = left_ref.shape[0]
    cols = new_ref.shape[1]
    left_ref[...] = jnp.zeros_like(left_ref)
    right_ref[...] = jnp.zeros_like(right_ref)
    updated = [r for start, count in runs_of(SECOND, rows) for r in range(start, start + count)]
    for k, r in enumerate(updated):
        left_ref[r : r + 1] = new_ref[k, :TILE].astype(F32)[:1]
        right_ref[r : r + 1] = new_ref[k, cols - TILE :].astype(F32)[TILE - 1 :]


def early_sides(rows, new):
    side = jax.ShapeDtypeStruct((rows, new.shape[2]), F32)
    return pl.pallas_call(
        early_sides_kernel,
        out_shape=(side, side),
        in_specs=[VMEM],
        out_specs=(VMEM, VMEM),
        compiler_params=params(LATE_BYTES),
        name="early_sides",
    )(new)


def exchange(value, axis, bit):
    return lax.ppermute(value, axis, [(i, i ^ bit) for i in range(lax.axis_size(axis))])


def across_groups(value):
    return exchange(value, "grp", 1)


def to_owners(value):
    return lax.all_to_all(value, ("lat", "lon"), split_axis=0, concat_axis=0, tiled=True)


def rows_beside(top, bottom):
    lats = lax.axis_size("lat")
    above = lax.ppermute(bottom, "lat", [(i, i + 1) for i in range(lats - 1)])
    below = lax.ppermute(top, "lat", [(i + 1, i) for i in range(lats - 1)])
    return above, below


def columns_beside(west, east):
    lons = lax.axis_size("lon")
    before = lax.ppermute(east, "lon", [(i, (i + 1) % lons) for i in range(lons)])
    after = lax.ppermute(west, "lon", [((i + 1) % lons, i) for i in range(lons)])
    return before, after


def body(
    state,
    intersection_lists,
    intersection_matrices,
    water,
    air_kernels,
    sea_kernels,
    flux_projection,
    coupling_matrix,
):
    current = state[0]
    rows = current.shape[0]
    tiles = lax.axis_size("lat") * lax.axis_size("lon")
    entries = intersection_lists.shape[-1]
    matrices = intersection_matrices.reshape(entries, BLOCK, BLOCK)

    first, second, lists, top, bottom, left, right = payloads(
        intersection_lists, current, matrices, water, flux_projection, tiles
    )
    first = across_groups(first)
    second = to_owners(second)
    halo_rows = rows_beside(top, bottom)
    middle = rows // 2
    summed, token = conv_inside(0, 0, middle, current, left, air_kernels, sea_kernels, False)
    first, west, east = pack(tiles, across_groups(lists), first, *halo_rows, left, right, token)
    first = to_owners(first)
    second = across_groups(second)
    halo = halo_rows + columns_beside(west, east)
    summed, held = conv_inside(0, middle, rows, current, summed, air_kernels, sea_kernels, True)
    summed = add_edges(0, summed, halo, air_kernels, sea_kernels)

    labels = slot_labels(second)
    early, top, bottom = update(SECOND, labels, second, summed, water, coupling_matrix)
    halo_rows = rows_beside(top, bottom)
    current, west, east = update(
        FIRST, labels, first, summed, water, coupling_matrix, (early, *halo_rows, *early_sides(rows, early))
    )
    beside = columns_beside(west, east)
    out, sides = last_conv(current, *halo_rows, water, held)
    out = fix_sides(out, sides, beside, water, held)
    return out[None]


def solution(mesh):
    placed = (
        P("grp", "lat", "lon", None),
        P("grp", "lat", "lon", None, None),
        P("grp", "lat", "lon", None, None, None),
        P("lat", "lon"),
        P(),
        P(),
        P(),
        P(),
    )
    return jax.shard_map(
        body, mesh=mesh, in_specs=placed, out_specs=P("grp", "lat", "lon", None), check_vma=False
    )
```

```python
import functools

import jax
import jax.numpy as jnp
from jax import lax
from jax.experimental import pallas as pl
from jax.experimental.pallas import tpu as pltpu
from jax.sharding import PartitionSpec as P

BLOCK_ROWS = 8
BLOCK_COLS = 16
BLOCK = BLOCK_ROWS * BLOCK_COLS
SLOTS = 2
FIRST = (1, 2, 3, 4, 5, 6)
SECOND = (0, 7)
FIRST_CELLS = len(FIRST) * BLOCK_COLS
SECOND_CELLS = len(SECOND) * BLOCK_COLS
LABEL_ROWS = 16
LANES = 128
VMEM_BYTES = 62 * 2**20
LATE_BYTES = 36 * 2**20
UPDATE_BYTES = 36 * 2**20

F32 = jnp.float32
BF16 = jnp.bfloat16

VMEM = pl.BlockSpec(memory_space=pltpu.VMEM)
SMEM = pl.BlockSpec(memory_space=pltpu.SMEM)
HBM = pl.BlockSpec(memory_space=pltpu.HBM)
ANY = pl.BlockSpec(memory_space=pl.ANY)


def silu(v):
    h = 0.5 * v
    return h + h * jnp.tanh(h)


def iota(shape, dim):
    return lax.broadcasted_iota(jnp.int32, shape, dim)


def dot(a, b):
    return jnp.dot(a, b, preferred_element_type=F32)


def params(limit=VMEM_BYTES):
    return pltpu.CompilerParams(vmem_limit_bytes=limit)


def on_ocean():
    return lax.axis_index("grp") == 1


def fill_water(water_ref, wide_ref, turned_ref):
    rows, longitudes = water_ref.shape
    wide_ref[:, 0:rows] = water_ref[...].astype(F32).T
    for p in range(2):
        turned_ref[:, p * rows : (p + 1) * rows] = wide_ref[pl.ds(p, longitudes // 2, stride=2), :][:, 0:rows]


def water_scratch(cols):
    return [pltpu.VMEM((2 * cols, 128), F32), pltpu.VMEM((cols, 128), F32)]


def water_of_row(turned_ref, rows, r, width, start, size):
    parts = [
        jnp.broadcast_to(turned_ref[start : start + size, p * rows + r : p * rows + r + 1], (size, width))
        for p in range(2)
    ]
    return jnp.concatenate(parts, axis=1)


def rim_shapes(rows, cols, width):
    line = jax.ShapeDtypeStruct((cols, width), BF16)
    side = jax.ShapeDtypeStruct((rows, width), F32)
    return (line, line, side, side)


def put_rim(rim, r, rows, line):
    top_ref, bottom_ref, left_ref, right_ref = rim
    cols = line.shape[0]
    exact = line.astype(F32)
    left_ref[r : r + 1] = exact[0:1]
    right_ref[r : r + 1] = exact[cols - 1 : cols]
    if r == 0:
        top_ref[...] = line
    if r == rows - 1:
        bottom_ref[...] = line


def payload_kernel(
    lists_in, state_hbm, matrices_hbm, water_ref, flux_hbm,
    first_ref, second_ref, lists_out, top_ref, bottom_ref, left_ref, right_ref,
    state_ref, matrices_ref, weights, flux_ref, flux, surface, wide_water, turned, count, sems,
):
    rows, cols, width = state_ref.shape
    half = width // 2
    entries = matrices_ref.shape[0]
    tiles = second_ref.shape[0]
    ocean = on_ocean()
    pieces = 4
    step = rows // pieces
    flux_copy = pltpu.make_async_copy(flux_hbm, flux_ref, sems.at[pieces])
    matrices_copy = pltpu.make_async_copy(matrices_hbm, matrices_ref, sems.at[pieces + 1])
    state_copies = [
        pltpu.make_async_copy(state_hbm.at[pl.ds(k * step, step)], state_ref.at[pl.ds(k * step, step)], sems.at[k])
        for k in range(pieces)
    ]
    lists_ref = lists_in.at[0, 0, 0]
    matrices_copy.start()
    flux_copy.start()
    for copy in state_copies:
        copy.start()

    def clear(t, _):
        count[t] = 0
        return 0

    lax.fori_loop(0, tiles, clear, 0)

    def keep(e, _):
        for k in range(3):
            lists_out[k, e] = lists_ref[k, e]
        return 0

    lax.fori_loop(0, entries, keep, 0)
    second_ref[:, SLOTS * SECOND_CELLS :, :] = jnp.full((tiles, LABEL_ROWS, half), -1.0, BF16)
    i = iota((BLOCK, BLOCK), 0)
    j = iota((BLOCK, BLOCK), 1)

    def put(e, payload, cut):
        owner = lists_ref[0, e]
        rank = count[owner]
        count[owner] = rank + 1
        first_ref[e], second = cut(payload)
        at = pl.multiple_of(rank * SECOND_CELLS, BLOCK_COLS)
        second_ref[owner, pl.ds(at, SECOND_CELLS), :] = second
        label = jnp.full((LABEL_ROWS, LANES), lists_ref[2, e], jnp.int32).astype(F32).astype(BF16)
        second_ref[owner, SLOTS * SECOND_CELLS :, pl.ds(pl.multiple_of(rank * LANES, LANES), LANES)] = label

    matrices_copy.wait()
    flux_copy.wait()

    @pl.when(jnp.logical_not(ocean))
    def _():
        wide = BLOCK_COLS // 2
        c = i % wide
        p1, r1 = i // (FIRST_CELLS // 2), FIRST[0] + i % (FIRST_CELLS // 2) // wide
        k = i - FIRST_CELLS
        q = k % (SECOND_CELLS // 2) // wide
        p2, r2 = k // (SECOND_CELLS // 2), jnp.where(q == 0, 0, q + FIRST[-1])
        p, r = jnp.where(k < 0, p1, p2), jnp.where(k < 0, r1, r2)
        turn = (j == r * BLOCK_COLS + 2 * c + p).astype(BF16)
        for e in range(entries):
            weights[e] = dot(turn, matrices_ref[e]).astype(BF16)
        for k in range(pieces):
            state_copies[k].wait()
            block = state_ref[k * step : (k + 1) * step].reshape(step * cols, width)
            flux[k * step : (k + 1) * step] = (
                dot(block, flux_ref[...]).astype(BF16).reshape(step, cols, half)
            )
        across = cols // BLOCK_COLS

        def entry(e, _):
            source = lists_ref[1, e]
            r0 = (source // across) * BLOCK_ROWS
            c0 = pl.multiple_of((source % across) * BLOCK_COLS, BLOCK_COLS)
            chosen = flux[pl.ds(r0, BLOCK_ROWS), pl.ds(c0, BLOCK_COLS), :].reshape(BLOCK, half)
            put(e, dot(weights[e], chosen).astype(BF16), lambda v: (v[:FIRST_CELLS], v[FIRST_CELLS:]))
            return 0

        lax.fori_loop(0, entries, entry, 0, unroll=8)

    @pl.when(ocean)
    def _():
        p, r, c = j // 64, (j // 8) % 8, j % 8
        turn = (i == r * BLOCK_COLS + 2 * c + p).astype(BF16)
        for e in range(entries):
            weights[e] = dot(matrices_ref[e], turn).astype(BF16)
        fill_water(water_ref, wide_water, turned)
        for k in range(pieces):
            state_copies[k].wait()
            for r0 in range(k * step, (k + 1) * step):
                surface[r0] = state_ref[r0].astype(F32) * water_of_row(turned, rows, r0, half, 0, cols)
        wide = BLOCK_COLS // 2
        across = cols // wide

        def entry(e, _):
            source = lists_ref[1, e]
            r0 = (source // across) * BLOCK_ROWS
            c0 = pl.multiple_of((source % across) * wide, wide)
            block = surface[pl.ds(r0, BLOCK_ROWS), pl.ds(c0, wide), :]
            chosen = jnp.concatenate(
                [block[:, :, q * half : (q + 1) * half].reshape(BLOCK // 2, half) for q in range(2)], axis=0
            ).astype(BF16)
            low, high = BLOCK_COLS, BLOCK_COLS + FIRST_CELLS
            put(
                e,
                dot(weights[e], chosen).astype(BF16),
                lambda v: (v[low:high], jnp.concatenate([v[:low], v[high:]], axis=0)),
            )
            return 0

        lax.fori_loop(0, entries, entry, 0, unroll=8)

    for r in range(rows):
        put_rim((top_ref, bottom_ref, left_ref, right_ref), r, rows, state_ref[r])


def payloads(lists, state, matrices, water, flux_projection, tiles):
    rows, cols, width = state.shape
    half = width // 2
    entries = lists.shape[-1]
    return pl.pallas_call(
        payload_kernel,
        out_shape=(
            jax.ShapeDtypeStruct((entries, FIRST_CELLS, half), BF16),
            jax.ShapeDtypeStruct((tiles, SLOTS * SECOND_CELLS + LABEL_ROWS, half), BF16),
            jax.ShapeDtypeStruct((3, entries), jnp.int32),
        )
        + rim_shapes(rows, cols, width),
        in_specs=[SMEM, HBM, HBM, VMEM, HBM],
        out_specs=(VMEM, VMEM, SMEM) + (VMEM,) * 4,
        scratch_shapes=[
            pltpu.VMEM(state.shape, BF16),
            pltpu.VMEM(matrices.shape, BF16),
            pltpu.VMEM(matrices.shape, BF16),
            pltpu.VMEM(flux_projection.shape, BF16),
            pltpu.VMEM((rows, cols, half), BF16),
            pltpu.VMEM((rows, cols, width), F32),
        ]
        + water_scratch(cols)
        + [
            pltpu.SMEM((tiles,), jnp.int32),
            pltpu.SemaphoreType.DMA((6,)),
        ],
        compiler_params=params(),
        name="payload",
    )(lists, state, matrices, water, flux_projection)


def pack_kernel(
    lists_ref, dense_ref, above_ref, below_ref, left_ref, right_ref, token_ref, slots_ref, west_ref, east_ref, count
):
    entries = lists_ref.shape[1]
    tiles = slots_ref.shape[0]

    def clear(t, _):
        count[t] = 0
        return 0

    lax.fori_loop(0, tiles, clear, 0)

    def place(e, _):
        owner = lists_ref[0, e]
        rank = count[owner]
        count[owner] = rank + 1
        at = pl.multiple_of(rank * FIRST_CELLS, BLOCK_COLS)
        slots_ref[owner, pl.ds(at, FIRST_CELLS), :] = dense_ref[e]
        return 0

    lax.fori_loop(0, entries, place, 0, unroll=4)
    del token_ref
    put_sides(above_ref, below_ref, left_ref, right_ref, west_ref, east_ref)


def pack(tiles, lists, dense, above, below, left, right, token):
    rows, width = left.shape
    side = jax.ShapeDtypeStruct((rows + 2, width), F32)
    return pl.pallas_call(
        pack_kernel,
        out_shape=(jax.ShapeDtypeStruct((tiles, SLOTS * FIRST_CELLS, dense.shape[2]), BF16), side, side),
        in_specs=[SMEM] + [VMEM] * 5 + [HBM],
        out_specs=(VMEM,) * 3,
        scratch_shapes=[pltpu.SMEM((tiles,), jnp.int32)],
        compiler_params=params(),
        name="pack",
    )(lists, dense, above, below, left, right, token)


def put_sides(above_ref, below_ref, left_ref, right_ref, west_ref, east_ref):
    rows = left_ref.shape[0]
    cols = above_ref.shape[0]
    for ref, side, at in ((west_ref, left_ref, 0), (east_ref, right_ref, cols - 1)):
        ref[0:1] = above_ref[at : at + 1].astype(F32)
        ref[1 : rows + 1] = side[...]
        ref[rows + 1 : rows + 2] = below_ref[at : at + 1].astype(F32)


def slot_labels(second):
    return second[:, SLOTS * SECOND_CELLS, ::LANES][:, :SLOTS].astype(jnp.int32).reshape(-1)


GROUP = 4


TILE = 8


def set_columns(line, before, after):
    cols = line.shape[0]
    left, right = pltpu.roll(line, 1, 0), pltpu.roll(line, cols - 1, 0)
    at = iota((TILE, line.shape[1]), 0)
    head = jnp.where(at == 0, before, left[:TILE])
    tail = jnp.where(at == TILE - 1, after, right[cols - TILE :])
    left = jnp.concatenate([head, left[TILE:]], axis=0)
    right = jnp.concatenate([right[: cols - TILE], tail], axis=0)
    return left, right


def air_line(h, before, after):
    left, right = set_columns(h, before, after)
    return jnp.concatenate([left, h, right], axis=1).astype(BF16)


def sea_line(h, before, after):
    half = h.shape[1] // 2
    left, _ = set_columns(h[:, half:], before[:, half:], after[:, half:])
    _, right = set_columns(h[:, :half], before[:, :half], after[:, :half])
    return jnp.concatenate([left, h, right], axis=1).astype(BF16)


def air_product(block, kernel):
    return dot(block, kernel.reshape(-1, kernel.shape[-1]))


def sea_product(block, kernel):
    width = kernel.shape[-1]
    flat = kernel.reshape(-1, width)
    return jnp.concatenate(
        [dot(block[:, : 3 * width], flat), dot(block[:, width : 4 * width], flat)], axis=1
    )


def each_component(run, air, sea):
    ocean = on_ocean()

    @pl.when(jnp.logical_not(ocean))
    def _():
        run(air, air_line, air_product, False)

    @pl.when(ocean)
    def _():
        run(sea, sea_line, sea_product, True)


def held_weights(air_kernels):
    return [pltpu.VMEM(air_kernels.shape[1:], BF16), pltpu.SemaphoreType.DMA((3, 3))]


def fetch_weights(layer, kernels_hbm, held, sems, wanted):
    width = kernels_hbm.shape[-1]
    copies = {
        (d, c): pltpu.make_async_copy(
            kernels_hbm.at[layer, d, c], held.at[d, c, pl.ds(0, width), pl.ds(0, width)], sems.at[d, c]
        )
        for d, c in wanted
    }
    for copy in copies.values():
        copy.start()
    return copies


def inside_conv_kernel(layer, begin, end, keep, *refs):
    x_hbm, _, air_hbm, sea_hbm, out_hbm, last_out = refs[:6]
    x_ref, lined, out, held, weight_sems, x_sems, sems = refs[6:13]
    rows, cols, width = x_hbm.shape
    low, high = max(begin - 1, 0), min(end + 1, rows)
    groups = (end - begin) // GROUP
    early = begin + GROUP + 1
    spans = [(low, early), (early, high)]
    every = [(d, c) for d in range(3) for c in range(3)]
    kept_write = None
    if keep:
        kept, kept_sems, kept_sem = refs[13:]
        kept_write = pltpu.make_async_copy(kept, last_out, kept_sem)
    else:
        last_out[...] = jnp.zeros_like(last_out)

    def read(k):
        at = pl.ds(spans[k][0], spans[k][1] - spans[k][0])
        return pltpu.make_async_copy(x_hbm.at[at], x_ref.at[at], x_sems.at[k])

    def write(g):
        at = g * GROUP
        return pltpu.make_async_copy(
            out.at[pl.ds(at, GROUP)], out_hbm.at[pl.ds(begin + at, GROUP)], sems.at[g]
        )

    def run(kernels_hbm, make_line, product, masked):
        wide = (2 if masked else 3) * width
        size = width // 2 if masked else width
        none = jnp.zeros((1, width), F32)
        read(0).start()
        weights = fetch_weights(layer, kernels_hbm, held, weight_sems, every)
        read(1).start()
        later = fetch_weights(layer + 1, kernels_hbm, kept, kept_sems, every) if keep else {}

        def put(r):
            if 0 <= r < rows:
                line = make_line(silu(x_ref[r].astype(F32)), none, none)
            else:
                line = jnp.zeros((cols, wide), BF16)
            lined[r - begin + 1, :, 0:wide] = line

        read(0).wait()
        for r in range(begin - 1, early):
            put(r)
        for copy in weights.values():
            copy.wait()
        read(1).wait()
        for g in range(groups):
            r0 = begin + g * GROUP
            total = x_ref[r0 : r0 + GROUP].astype(F32).reshape(GROUP * cols, width)
            for d in range(3):
                at = r0 - begin + d
                block = lined[at : at + GROUP, :, 0:wide].reshape(GROUP * cols, wide)
                total = total + product(block, held[d, :, 0:size, 0:size])
            if g + 1 < groups:
                for r in range(r0 + GROUP + 1, r0 + 2 * GROUP + 1):
                    put(r)
            out[r0 - begin : r0 - begin + GROUP] = total.reshape(GROUP, cols, width)
            write(g).start()
            if keep and g == 0:
                for copy in later.values():
                    copy.wait()
                kept_write.start()

    each_component(run, air_hbm, sea_hbm)
    for g in range(groups):
        write(g).wait()
    if keep:
        kept_write.wait()


def last_conv_kernel(
    x_ref, above_ref, below_ref, water_ref, held, out_hbm, sides_ref, lined, out, wide_water, turned, sems
):
    rows, cols, width = x_ref.shape
    half = width // 2
    groups = rows // GROUP

    def write(g):
        at = pl.ds(g * GROUP, GROUP)
        return pltpu.make_async_copy(out.at[at], out_hbm.at[at], sems.at[g])

    def run(_, make_line, product, masked):
        wide = (2 if masked else 3) * width
        size = half if masked else width
        none = jnp.zeros((1, width), F32)

        def put(r):
            line = above_ref[...] if r < 0 else below_ref[...] if r == rows else x_ref[r]
            lined[r + 1, :, 0:wide] = make_line(silu(line.astype(F32)), none, none)

        if masked:
            fill_water(water_ref, wide_water, turned)
        for r in range(-1, GROUP + 1):
            put(r)
        for g in range(groups):
            r0 = g * GROUP
            total = x_ref[r0 : r0 + GROUP].astype(F32).reshape(GROUP * cols, width)
            for d in range(3):
                block = lined[r0 + d : r0 + d + GROUP, :, 0:wide].reshape(GROUP * cols, wide)
                total = total + product(block, held[d, :, 0:size, 0:size])
            if g + 1 < groups:
                for r in range(r0 + GROUP + 1, r0 + 2 * GROUP + 1):
                    put(r)
            total = total.reshape(GROUP, cols, width)
            for k in range(GROUP):
                r = r0 + k
                line = total[k]
                sides_ref[0, r] = line[:BLOCK_COLS]
                sides_ref[1, r] = line[cols - BLOCK_COLS :]
                if masked:
                    line = line * water_of_row(turned, rows, r, half, 0, cols)
                out[r] = line.astype(BF16)
            write(g).start()

    each_component(run, None, None)
    for g in range(groups):
        write(g).wait()


def last_conv(state, above, below, water, held):
    rows, cols, width = state.shape
    return pl.pallas_call(
        last_conv_kernel,
        out_shape=(
            jax.ShapeDtypeStruct(state.shape, BF16),
            jax.ShapeDtypeStruct((2, rows, BLOCK_COLS, width), F32),
        ),
        in_specs=[VMEM] * 5,
        out_specs=(HBM, VMEM),
        scratch_shapes=[
            pltpu.VMEM((rows + 2, cols, 3 * width), BF16),
            pltpu.VMEM((rows, cols, width), BF16),
        ]
        + water_scratch(cols)
        + [pltpu.SemaphoreType.DMA((rows // GROUP,))],
        compiler_params=params(LATE_BYTES),
        cost_estimate=conv_cost(state, rows),
        name="last_conv",
    )(state, above, below, water, held)


def conv_cost(state, rows):
    cells = rows * state.shape[1]
    width = state.shape[2]
    return pl.CostEstimate(
        flops=2 * 9 * cells * width * width,
        bytes_accessed=cells * width * 6 + 9 * width * width * 2,
        transcendentals=cells * width,
    )


def conv_inside(layer, begin, end, state, after, air_kernels, sea_kernels, keep):
    rows, cols, width = state.shape
    count = end - begin
    kernel_shape = air_kernels.shape[1:]
    scratch = [
        pltpu.VMEM(state.shape, BF16),
        pltpu.VMEM((count + 2, cols, 3 * width), BF16),
        pltpu.VMEM((count, cols, width), F32),
    ] + held_weights(air_kernels)
    scratch += [pltpu.SemaphoreType.DMA((2,)), pltpu.SemaphoreType.DMA((count // GROUP,))]
    if keep:
        scratch += held_weights(air_kernels) + [pltpu.SemaphoreType.DMA]
    return pl.pallas_call(
        functools.partial(inside_conv_kernel, layer, begin, end, keep),
        out_shape=(
            jax.ShapeDtypeStruct(state.shape, F32),
            jax.ShapeDtypeStruct(kernel_shape, BF16) if keep else jax.ShapeDtypeStruct((8, 128), F32),
        ),
        in_specs=[HBM] * 4,
        out_specs=(HBM, HBM if keep else VMEM),
        scratch_shapes=scratch,
        input_output_aliases={1: 0} if keep else {},
        compiler_params=params(),
        cost_estimate=conv_cost(state, count),
        name="conv_inside",
    )(state, after, air_kernels, sea_kernels)


EDGE_WEIGHTS = [(0, 0), (1, 0), (2, 0), (0, 2), (1, 2), (2, 2), (0, 1), (2, 1)]


def halo_columns(rows, left_ref, right_ref, weights, held, masked):
    before = silu(left_ref[...])
    after = silu(right_ref[...])
    half = before.shape[1] // 2
    if masked:
        before, after = before[:, half:], after[:, :half]
    west = jnp.zeros((rows, before.shape[1]), F32)
    east = jnp.zeros((rows, before.shape[1]), F32)
    size = before.shape[1]
    for d in range(3):
        if weights:
            weights[d, 0].wait()
        west = west + dot(before[d : d + rows].astype(BF16), held[d, 0, 0:size, 0:size])
    for d in range(3):
        if weights:
            weights[d, 2].wait()
        east = east + dot(after[d : d + rows].astype(BF16), held[d, 2, 0:size, 0:size])
    if masked:
        blank = jnp.zeros((rows, half), F32)
        west = jnp.concatenate([west, blank], axis=1)
        east = jnp.concatenate([blank, east], axis=1)
    return west, east


def side_kernel(
    out_in_hbm, sides_ref, left_ref, right_ref, water_ref, held, out_hbm, side_out, wide_water, turned, sems,
):
    del out_in_hbm
    rows, cols, width = out_hbm.shape
    half = width // 2
    writes = [
        pltpu.make_async_copy(side_out.at[k], out_hbm.at[:, pl.ds(start, BLOCK_COLS)], sems.at[k])
        for k, start in enumerate((0, cols - BLOCK_COLS))
    ]

    def run(_, make_line, product, masked):
        if masked:
            fill_water(water_ref, wide_water, turned)
        added = halo_columns(rows, left_ref, right_ref, None, held, masked)
        at = iota((BLOCK_COLS, width), 0)
        for k, (start, here) in enumerate(((0, 0), (cols - BLOCK_COLS, BLOCK_COLS - 1))):
            for r in range(rows):
                total = sides_ref[k, r] + jnp.where(at == here, added[k][r : r + 1], 0.0)
                if masked:
                    total = total * water_of_row(turned, rows, r, half, start, BLOCK_COLS)
                side_out[k, r] = total.astype(BF16)
            writes[k].start()

    each_component(run, None, None)
    for copy in writes:
        copy.wait()


def fix_sides(out, sides, beside, water, held):
    rows, cols, width = out.shape
    return pl.pallas_call(
        side_kernel,
        out_shape=jax.ShapeDtypeStruct(out.shape, BF16),
        in_specs=[HBM] + [VMEM] * 5,
        out_specs=HBM,
        scratch_shapes=[pltpu.VMEM((2, rows, BLOCK_COLS, width), BF16)]
        + water_scratch(cols)
        + [pltpu.SemaphoreType.DMA((2,))],
        input_output_aliases={0: 0},
        compiler_params=params(LATE_BYTES),
        name="fix_sides",
    )(out, sides, *beside, water, held)


def edge_copies(rows, cols, count, lines, sides, hbm, sems, inward):
    inner = pl.ds(1, rows - 2)
    pairs = [
        (lines.at[0], hbm.at[0]),
        (lines.at[1], hbm.at[rows - 1]),
        (sides.at[0], hbm.at[inner, pl.ds(0, count)]),
        (sides.at[1], hbm.at[inner, pl.ds(cols - count, count)]),
    ]
    return [
        pltpu.make_async_copy(*(pair[::-1] if inward else pair), sems.at[k]) for k, pair in enumerate(pairs)
    ]


SIDE = 8


def sum_edge_kernel(
    layer, sum_in_hbm, top_ref, bottom_ref, left_ref, right_ref, air_hbm, sea_hbm, sum_hbm,
    lines, sides, held, weight_sems, read_sems, sems,
):
    rows, cols, width = sum_hbm.shape
    reads = edge_copies(rows, cols, SIDE, lines, sides, sum_in_hbm, read_sems, True)
    writes = edge_copies(rows, cols, SIDE, lines, sides, sum_hbm, sems, False)
    for copy in reads:
        copy.start()

    def run(kernels_hbm, make_line, product, masked):
        size = width // 2 if masked else width
        weights = fetch_weights(layer, kernels_hbm, held, weight_sems, EDGE_WEIGHTS)
        none = jnp.zeros((1, width), F32)
        west, east = halo_columns(rows, left_ref, right_ref, weights, held, masked)
        for copy in reads:
            copy.wait()
        at = iota((SIDE, width), 0)
        for r in range(1, rows - 1):
            sides[0, r - 1] += jnp.where(at == 0, west[r : r + 1], 0.0)
            sides[1, r - 1] += jnp.where(at == SIDE - 1, east[r : r + 1], 0.0)
        at = iota((cols, width), 0)
        for k, (line, d) in enumerate(((top_ref, 0), (bottom_ref, 2))):
            r = 0 if k == 0 else rows - 1
            lined = make_line(silu(line[...].astype(F32)), none, none)
            weights[d, 1].wait()
            total = lines[k] + product(lined, held[d, :, 0:size, 0:size])
            total = total + jnp.where(at == 0, west[r : r + 1], 0.0)
            lines[k] = total + jnp.where(at == cols - 1, east[r : r + 1], 0.0)

    each_component(run, air_hbm, sea_hbm)
    for copy in writes:
        copy.start()
    for copy in writes:
        copy.wait()


def add_edges(layer, summed, halo, air_kernels, sea_kernels):
    rows, cols, width = summed.shape
    return pl.pallas_call(
        functools.partial(sum_edge_kernel, layer),
        out_shape=jax.ShapeDtypeStruct(summed.shape, F32),
        in_specs=[HBM] + [VMEM] * 4 + [HBM] * 2,
        out_specs=HBM,
        scratch_shapes=[
            pltpu.VMEM((2, cols, width), F32),
            pltpu.VMEM((2, rows - 2, SIDE, width), F32),
        ]
        + held_weights(air_kernels)
        + [pltpu.SemaphoreType.DMA((4,)), pltpu.SemaphoreType.DMA((4,))],
        input_output_aliases={0: 0},
        compiler_params=params(),
        name="add_edges",
    )(summed, *halo, air_kernels, sea_kernels)


def runs_of(block_rows, rows):
    runs = []
    for r in range(rows):
        if r % BLOCK_ROWS in block_rows:
            if runs and sum(runs[-1]) == r:
                runs[-1] = (runs[-1][0], runs[-1][1] + 1)
            else:
                runs.append((r, 1))
    return runs


def update_kernel(block_rows, last, *refs):
    if last:
        (labels_ref, message_hbm, sum_hbm, water_ref, coupling_hbm, early_new, above_ref, below_ref) = refs[:8]
        (early_left, early_right, new_ref, west_ref, east_ref) = refs[8:13]
        refs = refs[13:]
        left_ref, right_ref, refs = refs[0], refs[1], refs[2:]
    else:
        (labels_ref, message_hbm, sum_hbm, water_ref, coupling_hbm) = refs[:5]
        new_ref, top_ref, bottom_ref = refs[5:8]
        refs = refs[8:]
    (total, message, sum_ref, coupling_ref, wide_water, turned) = refs[:6]
    (message_sem, coupling_sem, sum_sems) = refs[6:]
    rows, cols, width = sum_ref.shape
    half = width // 2
    slots = message_hbm.shape[0] * SLOTS
    cells = len(block_rows) * BLOCK_COLS
    runs = runs_of(block_rows, rows)
    parts = [(start, count, block_rows.index(start)) for start, count in runs_of(block_rows, BLOCK_ROWS)]
    updated = [r for start, count in runs for r in range(start, start + count)]
    ocean = on_ocean()

    def run_copy(source, target, k, sems):
        at = pl.ds(*runs[k])
        return pltpu.make_async_copy(source.at[at], target.at[at], sems.at[k])

    message_copy = pltpu.make_async_copy(message_hbm, message, message_sem)
    coupling_copy = pltpu.make_async_copy(coupling_hbm, coupling_ref, coupling_sem)
    message_copy.start()
    for k in range(len(runs)):
        run_copy(sum_hbm, sum_ref, k, sum_sems).start()
    coupling_copy.start()
    if last:
        at = 0
        for start, count in runs_of([r for r in range(BLOCK_ROWS) if r not in block_rows], rows):
            new_ref[start : start + count] = early_new[at : at + count]
            at += count
        left_ref[...] = early_left[...]
        right_ref[...] = early_right[...]

    def clear(lanes):
        for start, count in runs:
            total[start : start + count, :, 0:lanes] = jnp.zeros((count, cols, lanes), F32)

    def each_slot(act):
        def one(s, _):
            label = labels_ref[s]

            @pl.when(label >= 0)
            def _():
                at = pl.multiple_of((s % SLOTS) * cells, BLOCK_COLS)
                act(message[s // SLOTS, pl.ds(at, cells), :].astype(F32), label)

            return 0

        lax.fori_loop(0, slots, one, 0)

    def store(r, line):
        low = line.astype(BF16)
        new_ref[r if last else updated.index(r)] = low
        if last:
            left_ref[r : r + 1] = low[:TILE].astype(F32)[:1]
            right_ref[r : r + 1] = low[cols - TILE :].astype(F32)[TILE - 1 :]
        elif r == 0:
            top_ref[...] = low
        elif r == rows - 1:
            bottom_ref[...] = low

    @pl.when(jnp.logical_not(ocean))
    def _():
        clear(half)
        across = cols // BLOCK_COLS

        def add(value, label):
            r0 = (label // across) * BLOCK_ROWS
            c0 = pl.multiple_of((label % across) * BLOCK_COLS, BLOCK_COLS)
            value = value.reshape(len(block_rows), BLOCK_COLS, half)
            for start, count, at in parts:
                total[pl.ds(r0 + start, count), pl.ds(c0, BLOCK_COLS), 0:half] += value[at : at + count]

        message_copy.wait()
        each_slot(add)
        coupling_copy.wait()
        for k, (start, count) in enumerate(runs):
            block = total[start : start + count, :, 0:half].astype(BF16).reshape(count * cols, half)
            force = dot(block, coupling_ref[...]).reshape(count, cols, width)
            run_copy(sum_hbm, sum_ref, k, sum_sems).wait()
            for q in range(count):
                store(start + q, sum_ref[start + q] + force[q])

    @pl.when(ocean)
    def _():
        clear(width)
        fill_water(water_ref, wide_water, turned)
        wide = BLOCK_COLS // 2
        across = cols // wide

        def add(value, label):
            r0 = (label // across) * BLOCK_ROWS
            c0 = pl.multiple_of((label % across) * wide, wide)
            value = value.reshape(2, len(block_rows), wide, half)
            for start, count, at in parts:
                for p in range(2):
                    lanes = slice(p * half, (p + 1) * half)
                    total[pl.ds(r0 + start, count), pl.ds(c0, wide), lanes] += value[p, at : at + count]

        message_copy.wait()
        each_slot(add)
        coupling_copy.wait()
        for k, (start, count) in enumerate(runs):
            run_copy(sum_hbm, sum_ref, k, sum_sems).wait()
            for r in range(start, start + count):
                store(r, (sum_ref[r] + total[r]) * water_of_row(turned, rows, r, half, 0, cols))

    if last:
        put_sides(above_ref, below_ref, left_ref, right_ref, west_ref, east_ref)


def update(block_rows, labels, message, summed, water, coupling_matrix, early=None):
    rows, cols, width = summed.shape
    last = early is not None
    side = jax.ShapeDtypeStruct((rows + 2, width), F32)
    runs = len(runs_of(block_rows, rows))
    count = rows if last else rows // BLOCK_ROWS * len(block_rows)
    kept = [pltpu.VMEM((rows, width), F32)] * 2 if last else []
    return pl.pallas_call(
        functools.partial(update_kernel, block_rows, last),
        out_shape=(jax.ShapeDtypeStruct((count, cols, width), BF16),)
        + ((side, side) if last else rim_shapes(rows, cols, width)[:2]),
        in_specs=[SMEM, HBM, HBM, VMEM, HBM] + ([VMEM] * 5 if last else []),
        out_specs=(VMEM,) * 3,
        scratch_shapes=kept
        + [
            pltpu.VMEM((rows, cols, width), F32),
            pltpu.VMEM(message.shape, BF16),
            pltpu.VMEM((rows, cols, width), F32),
            pltpu.VMEM(coupling_matrix.shape, BF16),
        ]
        + water_scratch(cols)
        + [
            pltpu.SemaphoreType.DMA,
            pltpu.SemaphoreType.DMA,
            pltpu.SemaphoreType.DMA((runs,)),
        ],
        compiler_params=params(UPDATE_BYTES if last else VMEM_BYTES),
        name="update",
    )(labels, message, summed, water, coupling_matrix, *(early or ()))


def early_sides_kernel(new_ref, _, __, left_ref, right_ref, ___):
    rows = left_ref.shape[0]
    cols = new_ref.shape[1]
    left_ref[...] = jnp.zeros_like(left_ref)
    right_ref[...] = jnp.zeros_like(right_ref)
    updated = [r for start, count in runs_of(SECOND, rows) for r in range(start, start + count)]
    for k, r in enumerate(updated):
        left_ref[r : r + 1] = new_ref[k, :TILE].astype(F32)[:1]
        right_ref[r : r + 1] = new_ref[k, cols - TILE :].astype(F32)[TILE - 1 :]


def early_sides(rows, new, summed, coupling_matrix):
    side = jax.ShapeDtypeStruct((rows, new.shape[2]), F32)
    return pl.pallas_call(
        early_sides_kernel,
        out_shape=(side, side, jax.ShapeDtypeStruct(summed.shape, F32)),
        in_specs=[VMEM, ANY, ANY],
        out_specs=(VMEM, VMEM, ANY),
        input_output_aliases={1: 2},
        compiler_params=params(LATE_BYTES),
        name="early_sides",
    )(new, summed, coupling_matrix)


def exchange(value, axis, bit):
    return lax.ppermute(value, axis, [(i, i ^ bit) for i in range(lax.axis_size(axis))])


def across_groups(value):
    return exchange(value, "grp", 1)


def to_owners(value):
    return lax.all_to_all(value, ("lat", "lon"), split_axis=0, concat_axis=0, tiled=True)


def rows_beside(top, bottom):
    lats = lax.axis_size("lat")
    above = lax.ppermute(bottom, "lat", [(i, i + 1) for i in range(lats - 1)])
    below = lax.ppermute(top, "lat", [(i + 1, i) for i in range(lats - 1)])
    return above, below


def columns_beside(west, east):
    lons = lax.axis_size("lon")
    before = lax.ppermute(east, "lon", [(i, (i + 1) % lons) for i in range(lons)])
    after = lax.ppermute(west, "lon", [((i + 1) % lons, i) for i in range(lons)])
    return before, after


def body(
    state,
    intersection_lists,
    intersection_matrices,
    water,
    air_kernels,
    sea_kernels,
    flux_projection,
    coupling_matrix,
):
    current = state[0]
    rows = current.shape[0]
    tiles = lax.axis_size("lat") * lax.axis_size("lon")
    entries = intersection_lists.shape[-1]
    matrices = intersection_matrices.reshape(entries, BLOCK, BLOCK)

    first, second, lists, top, bottom, left, right = payloads(
        intersection_lists, current, matrices, water, flux_projection, tiles
    )
    first = across_groups(first)
    second = to_owners(second)
    halo_rows = rows_beside(top, bottom)
    middle = rows // 2
    summed, token = conv_inside(0, 0, middle, current, left, air_kernels, sea_kernels, False)
    first, west, east = pack(tiles, across_groups(lists), first, *halo_rows, left, right, token)
    first = to_owners(first)
    second = across_groups(second)
    halo = halo_rows + columns_beside(west, east)
    summed, held = conv_inside(0, middle, rows, current, summed, air_kernels, sea_kernels, True)
    summed = add_edges(0, summed, halo, air_kernels, sea_kernels)

    labels = slot_labels(second)
    early, top, bottom = update(SECOND, labels, second, summed, water, coupling_matrix)
    halo_rows = rows_beside(top, bottom)
    left, right, summed = early_sides(rows, early, summed, coupling_matrix)
    current, west, east = update(
        FIRST, labels, first, summed, water, coupling_matrix, (early, *halo_rows, left, right)
    )
    beside = columns_beside(west, east)
    out, sides = last_conv(current, *halo_rows, water, held)
    out = fix_sides(out, sides, beside, water, held)
    return out[None]


def solution(mesh):
    placed = (
        P("grp", "lat", "lon", None),
        P("grp", "lat", "lon", None, None),
        P("grp", "lat", "lon", None, None, None),
        P("lat", "lon"),
        P(),
        P(),
        P(),
        P(),
    )
    return jax.shard_map(
        body, mesh=mesh, in_specs=placed, out_specs=P("grp", "lat", "lon", None), check_vma=False
    )
```

```python
import functools

import jax
import jax.numpy as jnp
from jax import lax
from jax.experimental import pallas as pl
from jax.experimental.pallas import tpu as pltpu
from jax.sharding import PartitionSpec as P

BLOCK_ROWS = 8
BLOCK_COLS = 16
BLOCK = BLOCK_ROWS * BLOCK_COLS
SLOTS = 2
FIRST = (1, 2, 3, 4, 5, 6)
SECOND = (0, 7)
FIRST_CELLS = len(FIRST) * BLOCK_COLS
SECOND_CELLS = len(SECOND) * BLOCK_COLS
LABEL_ROWS = 16
LANES = 128
VMEM_BYTES = 61 * 2**20
LATE_BYTES = 36 * 2**20
UPDATE_BYTES = 36 * 2**20

F32 = jnp.float32
BF16 = jnp.bfloat16

VMEM = pl.BlockSpec(memory_space=pltpu.VMEM)
SMEM = pl.BlockSpec(memory_space=pltpu.SMEM)
HBM = pl.BlockSpec(memory_space=pltpu.HBM)
ANY = pl.BlockSpec(memory_space=pl.ANY)


def silu(v):
    h = 0.5 * v
    return h + h * jnp.tanh(h)


def iota(shape, dim):
    return lax.broadcasted_iota(jnp.int32, shape, dim)


def dot(a, b):
    return jnp.dot(a, b, preferred_element_type=F32)


def params(limit=VMEM_BYTES):
    return pltpu.CompilerParams(vmem_limit_bytes=limit)


def on_ocean():
    return lax.axis_index("grp") == 1


def fill_water(water_ref, wide_ref, turned_ref):
    rows, longitudes = water_ref.shape
    wide_ref[:, 0:rows] = water_ref[...].astype(F32).T
    for p in range(2):
        turned_ref[:, p * rows : (p + 1) * rows] = wide_ref[pl.ds(p, longitudes // 2, stride=2), :][:, 0:rows]


def water_scratch(cols):
    return [pltpu.VMEM((2 * cols, 128), F32), pltpu.VMEM((cols, 128), F32)]


def water_of_row(turned_ref, rows, r, width, start, size):
    parts = [
        jnp.broadcast_to(turned_ref[start : start + size, p * rows + r : p * rows + r + 1], (size, width))
        for p in range(2)
    ]
    return jnp.concatenate(parts, axis=1)


def rim_shapes(rows, cols, width):
    line = jax.ShapeDtypeStruct((cols, width), BF16)
    side = jax.ShapeDtypeStruct((rows, width), F32)
    return (line, line, side, side)


def put_rim(rim, r, rows, line):
    top_ref, bottom_ref, left_ref, right_ref = rim
    cols = line.shape[0]
    exact = line.astype(F32)
    left_ref[r : r + 1] = exact[0:1]
    right_ref[r : r + 1] = exact[cols - 1 : cols]
    if r == 0:
        top_ref[...] = line
    if r == rows - 1:
        bottom_ref[...] = line


def payload_kernel(
    lists_in, state_hbm, matrices_hbm, water_ref, flux_hbm,
    first_ref, second_ref, lists_out, top_ref, bottom_ref, left_ref, right_ref,
    state_ref, matrices_ref, weights, flux_ref, flux, surface, wide_water, turned, count, sems,
):
    rows, cols, width = state_ref.shape
    half = width // 2
    entries = matrices_ref.shape[0]
    tiles = second_ref.shape[0]
    ocean = on_ocean()
    pieces = 4
    step = rows // pieces
    flux_copy = pltpu.make_async_copy(flux_hbm, flux_ref, sems.at[pieces])
    matrices_copy = pltpu.make_async_copy(matrices_hbm, matrices_ref, sems.at[pieces + 1])
    state_copies = [
        pltpu.make_async_copy(state_hbm.at[pl.ds(k * step, step)], state_ref.at[pl.ds(k * step, step)], sems.at[k])
        for k in range(pieces)
    ]
    lists_ref = lists_in.at[0, 0, 0]
    matrices_copy.start()
    flux_copy.start()
    for copy in state_copies:
        copy.start()

    def clear(t, _):
        count[t] = 0
        return 0

    lax.fori_loop(0, tiles, clear, 0)

    def keep(e, _):
        for k in range(3):
            lists_out[k, e] = lists_ref[k, e]
        return 0

    lax.fori_loop(0, entries, keep, 0)
    second_ref[:, SLOTS * SECOND_CELLS :, :] = jnp.full((tiles, LABEL_ROWS, half), -1.0, BF16)
    i = iota((BLOCK, BLOCK), 0)
    j = iota((BLOCK, BLOCK), 1)

    def put(e, payload, cut):
        owner = lists_ref[0, e]
        rank = count[owner]
        count[owner] = rank + 1
        first_ref[e], second = cut(payload)
        at = pl.multiple_of(rank * SECOND_CELLS, BLOCK_COLS)
        second_ref[owner, pl.ds(at, SECOND_CELLS), :] = second
        label = jnp.full((LABEL_ROWS, LANES), lists_ref[2, e], jnp.int32).astype(F32).astype(BF16)
        second_ref[owner, SLOTS * SECOND_CELLS :, pl.ds(pl.multiple_of(rank * LANES, LANES), LANES)] = label

    matrices_copy.wait()
    flux_copy.wait()

    @pl.when(jnp.logical_not(ocean))
    def _():
        wide = BLOCK_COLS // 2
        c = i % wide
        p1, r1 = i // (FIRST_CELLS // 2), FIRST[0] + i % (FIRST_CELLS // 2) // wide
        k = i - FIRST_CELLS
        q = k % (SECOND_CELLS // 2) // wide
        p2, r2 = k // (SECOND_CELLS // 2), jnp.where(q == 0, 0, q + FIRST[-1])
        p, r = jnp.where(k < 0, p1, p2), jnp.where(k < 0, r1, r2)
        turn = (j == r * BLOCK_COLS + 2 * c + p).astype(BF16)
        for e in range(entries):
            weights[e] = dot(turn, matrices_ref[e]).astype(BF16)
        for k in range(pieces):
            state_copies[k].wait()
            block = state_ref[k * step : (k + 1) * step].reshape(step * cols, width)
            flux[k * step : (k + 1) * step] = (
                dot(block, flux_ref[...]).astype(BF16).reshape(step, cols, half)
            )
        across = cols // BLOCK_COLS

        def entry(e, _):
            source = lists_ref[1, e]
            r0 = (source // across) * BLOCK_ROWS
            c0 = pl.multiple_of((source % across) * BLOCK_COLS, BLOCK_COLS)
            chosen = flux[pl.ds(r0, BLOCK_ROWS), pl.ds(c0, BLOCK_COLS), :].reshape(BLOCK, half)
            put(e, dot(weights[e], chosen).astype(BF16), lambda v: (v[:FIRST_CELLS], v[FIRST_CELLS:]))
            return 0

        lax.fori_loop(0, entries, entry, 0, unroll=8)

    @pl.when(ocean)
    def _():
        p, r, c = j // 64, (j // 8) % 8, j % 8
        turn = (i == r * BLOCK_COLS + 2 * c + p).astype(BF16)
        for e in range(entries):
            weights[e] = dot(matrices_ref[e], turn).astype(BF16)
        fill_water(water_ref, wide_water, turned)
        for k in range(pieces):
            state_copies[k].wait()
            for r0 in range(k * step, (k + 1) * step):
                surface[r0] = state_ref[r0].astype(F32) * water_of_row(turned, rows, r0, half, 0, cols)
        wide = BLOCK_COLS // 2
        across = cols // wide

        def entry(e, _):
            source = lists_ref[1, e]
            r0 = (source // across) * BLOCK_ROWS
            c0 = pl.multiple_of((source % across) * wide, wide)
            block = surface[pl.ds(r0, BLOCK_ROWS), pl.ds(c0, wide), :]
            chosen = jnp.concatenate(
                [block[:, :, q * half : (q + 1) * half].reshape(BLOCK // 2, half) for q in range(2)], axis=0
            ).astype(BF16)
            low, high = BLOCK_COLS, BLOCK_COLS + FIRST_CELLS
            put(
                e,
                dot(weights[e], chosen).astype(BF16),
                lambda v: (v[low:high], jnp.concatenate([v[:low], v[high:]], axis=0)),
            )
            return 0

        lax.fori_loop(0, entries, entry, 0, unroll=8)

    for r in range(rows):
        put_rim((top_ref, bottom_ref, left_ref, right_ref), r, rows, state_ref[r])


def payloads(lists, state, matrices, water, flux_projection, tiles):
    rows, cols, width = state.shape
    half = width // 2
    entries = lists.shape[-1]
    return pl.pallas_call(
        payload_kernel,
        out_shape=(
            jax.ShapeDtypeStruct((entries, FIRST_CELLS, half), BF16),
            jax.ShapeDtypeStruct((tiles, SLOTS * SECOND_CELLS + LABEL_ROWS, half), BF16),
            jax.ShapeDtypeStruct((3, entries), jnp.int32),
        )
        + rim_shapes(rows, cols, width),
        in_specs=[SMEM, HBM, HBM, VMEM, HBM],
        out_specs=(VMEM, VMEM, SMEM) + (VMEM,) * 4,
        scratch_shapes=[
            pltpu.VMEM(state.shape, BF16),
            pltpu.VMEM(matrices.shape, BF16),
            pltpu.VMEM(matrices.shape, BF16),
            pltpu.VMEM(flux_projection.shape, BF16),
            pltpu.VMEM((rows, cols, half), BF16),
            pltpu.VMEM((rows, cols, width), F32),
        ]
        + water_scratch(cols)
        + [
            pltpu.SMEM((tiles,), jnp.int32),
            pltpu.SemaphoreType.DMA((6,)),
        ],
        compiler_params=params(),
        name="payload",
    )(lists, state, matrices, water, flux_projection)


def pack_kernel(
    lists_ref, dense_ref, above_ref, below_ref, left_ref, right_ref, token_ref, slots_ref, west_ref, east_ref, count
):
    entries = lists_ref.shape[1]
    tiles = slots_ref.shape[0]

    def clear(t, _):
        count[t] = 0
        return 0

    lax.fori_loop(0, tiles, clear, 0)

    def place(e, _):
        owner = lists_ref[0, e]
        rank = count[owner]
        count[owner] = rank + 1
        at = pl.multiple_of(rank * FIRST_CELLS, BLOCK_COLS)
        slots_ref[owner, pl.ds(at, FIRST_CELLS), :] = dense_ref[e]
        return 0

    lax.fori_loop(0, entries, place, 0, unroll=4)
    del token_ref
    put_sides(above_ref, below_ref, left_ref, right_ref, west_ref, east_ref)


def pack(tiles, lists, dense, above, below, left, right, token):
    rows, width = left.shape
    side = jax.ShapeDtypeStruct((rows + 2, width), F32)
    return pl.pallas_call(
        pack_kernel,
        out_shape=(jax.ShapeDtypeStruct((tiles, SLOTS * FIRST_CELLS, dense.shape[2]), BF16), side, side),
        in_specs=[SMEM] + [VMEM] * 5 + [HBM],
        out_specs=(VMEM,) * 3,
        scratch_shapes=[pltpu.SMEM((tiles,), jnp.int32)],
        compiler_params=params(),
        name="pack",
    )(lists, dense, above, below, left, right, token)


def put_sides(above_ref, below_ref, left_ref, right_ref, west_ref, east_ref):
    rows = left_ref.shape[0]
    cols = above_ref.shape[0]
    for ref, side, at in ((west_ref, left_ref, 0), (east_ref, right_ref, cols - 1)):
        ref[0:1] = above_ref[at : at + 1].astype(F32)
        ref[1 : rows + 1] = side[...]
        ref[rows + 1 : rows + 2] = below_ref[at : at + 1].astype(F32)


def slot_labels(second):
    return second[:, SLOTS * SECOND_CELLS, ::LANES][:, :SLOTS].astype(jnp.int32).reshape(-1)


GROUP = 4


TILE = 8


def set_columns(line, before, after):
    cols = line.shape[0]
    left, right = pltpu.roll(line, 1, 0), pltpu.roll(line, cols - 1, 0)
    at = iota((TILE, line.shape[1]), 0)
    head = jnp.where(at == 0, before, left[:TILE])
    tail = jnp.where(at == TILE - 1, after, right[cols - TILE :])
    left = jnp.concatenate([head, left[TILE:]], axis=0)
    right = jnp.concatenate([right[: cols - TILE], tail], axis=0)
    return left, right


def air_line(h, before, after):
    left, right = set_columns(h, before, after)
    return jnp.concatenate([left, h, right], axis=1).astype(BF16)


def sea_line(h, before, after):
    half = h.shape[1] // 2
    left, _ = set_columns(h[:, half:], before[:, half:], after[:, half:])
    _, right = set_columns(h[:, :half], before[:, :half], after[:, :half])
    return jnp.concatenate([left, h, right], axis=1).astype(BF16)


def air_product(block, kernel):
    return dot(block, kernel.reshape(-1, kernel.shape[-1]))


def sea_product(block, kernel):
    width = kernel.shape[-1]
    flat = kernel.reshape(-1, width)
    return jnp.concatenate(
        [dot(block[:, : 3 * width], flat), dot(block[:, width : 4 * width], flat)], axis=1
    )


def each_component(run, air, sea):
    ocean = on_ocean()

    @pl.when(jnp.logical_not(ocean))
    def _():
        run(air, air_line, air_product, False)

    @pl.when(ocean)
    def _():
        run(sea, sea_line, sea_product, True)


def held_weights(air_kernels):
    return [pltpu.VMEM(air_kernels.shape[1:], BF16), pltpu.SemaphoreType.DMA((3, 3))]


def fetch_weights(layer, kernels_hbm, held, sems, wanted):
    width = kernels_hbm.shape[-1]
    copies = {
        (d, c): pltpu.make_async_copy(
            kernels_hbm.at[layer, d, c], held.at[d, c, pl.ds(0, width), pl.ds(0, width)], sems.at[d, c]
        )
        for d, c in wanted
    }
    for copy in copies.values():
        copy.start()
    return copies


def inside_conv_kernel(layer, begin, end, keep, *refs):
    x_hbm, _, air_hbm, sea_hbm, out_hbm, last_out = refs[:6]
    x_ref, lined, out, held, weight_sems, x_sems, sems = refs[6:13]
    rows, cols, width = x_hbm.shape
    low, high = max(begin - 1, 0), min(end + 1, rows)
    groups = (end - begin) // GROUP
    early = begin + GROUP + 1
    spans = [(low, early), (early, high)]
    every = [(d, c) for d in range(3) for c in range(3)]
    kept_write = None
    if keep:
        kept, kept_sems, kept_sem = refs[13:]
        kept_write = pltpu.make_async_copy(kept, last_out, kept_sem)
    else:
        last_out[...] = jnp.zeros_like(last_out)

    def read(k):
        at = pl.ds(spans[k][0], spans[k][1] - spans[k][0])
        return pltpu.make_async_copy(x_hbm.at[at], x_ref.at[at], x_sems.at[k])

    def write(g):
        at = g * GROUP
        return pltpu.make_async_copy(
            out.at[pl.ds(at, GROUP)], out_hbm.at[pl.ds(begin + at, GROUP)], sems.at[g]
        )

    def run(kernels_hbm, make_line, product, masked):
        wide = (2 if masked else 3) * width
        size = width // 2 if masked else width
        none = jnp.zeros((1, width), F32)
        read(0).start()
        weights = fetch_weights(layer, kernels_hbm, held, weight_sems, every)
        read(1).start()
        later = fetch_weights(layer + 1, kernels_hbm, kept, kept_sems, every) if keep else {}

        def put(r):
            if 0 <= r < rows:
                line = make_line(silu(x_ref[r].astype(F32)), none, none)
            else:
                line = jnp.zeros((cols, wide), BF16)
            lined[r - begin + 1, :, 0:wide] = line

        read(0).wait()
        for r in range(begin - 1, early):
            put(r)
        for copy in weights.values():
            copy.wait()
        read(1).wait()
        for g in range(groups):
            r0 = begin + g * GROUP
            total = x_ref[r0 : r0 + GROUP].astype(F32).reshape(GROUP * cols, width)
            for d in range(3):
                at = r0 - begin + d
                block = lined[at : at + GROUP, :, 0:wide].reshape(GROUP * cols, wide)
                total = total + product(block, held[d, :, 0:size, 0:size])
            if g + 1 < groups:
                for r in range(r0 + GROUP + 1, r0 + 2 * GROUP + 1):
                    put(r)
            out[r0 - begin : r0 - begin + GROUP] = total.reshape(GROUP, cols, width)
            write(g).start()
            if keep and g == 0:
                for copy in later.values():
                    copy.wait()
                kept_write.start()

    each_component(run, air_hbm, sea_hbm)
    for g in range(groups):
        write(g).wait()
    if keep:
        kept_write.wait()


def last_conv_kernel(
    x_ref, above_ref, below_ref, water_ref, held, out_hbm, sides_ref, lined, out, wide_water, turned, sems
):
    rows, cols, width = x_ref.shape
    half = width // 2
    groups = rows // GROUP

    def write(g):
        at = pl.ds(g * GROUP, GROUP)
        return pltpu.make_async_copy(out.at[at], out_hbm.at[at], sems.at[g])

    def run(_, make_line, product, masked):
        wide = (2 if masked else 3) * width
        size = half if masked else width
        none = jnp.zeros((1, width), F32)

        def put(r):
            line = above_ref[...] if r < 0 else below_ref[...] if r == rows else x_ref[r]
            lined[r + 1, :, 0:wide] = make_line(silu(line.astype(F32)), none, none)

        if masked:
            fill_water(water_ref, wide_water, turned)
        for r in range(-1, GROUP + 1):
            put(r)
        for g in range(groups):
            r0 = g * GROUP
            total = x_ref[r0 : r0 + GROUP].astype(F32).reshape(GROUP * cols, width)
            for d in range(3):
                block = lined[r0 + d : r0 + d + GROUP, :, 0:wide].reshape(GROUP * cols, wide)
                total = total + product(block, held[d, :, 0:size, 0:size])
            if g + 1 < groups:
                for r in range(r0 + GROUP + 1, r0 + 2 * GROUP + 1):
                    put(r)
            total = total.reshape(GROUP, cols, width)
            for k in range(GROUP):
                r = r0 + k
                line = total[k]
                sides_ref[0, r] = line[:BLOCK_COLS]
                sides_ref[1, r] = line[cols - BLOCK_COLS :]
                if masked:
                    line = line * water_of_row(turned, rows, r, half, 0, cols)
                out[r] = line.astype(BF16)
            write(g).start()

    each_component(run, None, None)
    for g in range(groups):
        write(g).wait()


def last_conv(state, above, below, water, held):
    rows, cols, width = state.shape
    return pl.pallas_call(
        last_conv_kernel,
        out_shape=(
            jax.ShapeDtypeStruct(state.shape, BF16),
            jax.ShapeDtypeStruct((2, rows, BLOCK_COLS, width), F32),
        ),
        in_specs=[VMEM] * 5,
        out_specs=(HBM, VMEM),
        scratch_shapes=[
            pltpu.VMEM((rows + 2, cols, 3 * width), BF16),
            pltpu.VMEM((rows, cols, width), BF16),
        ]
        + water_scratch(cols)
        + [pltpu.SemaphoreType.DMA((rows // GROUP,))],
        compiler_params=params(LATE_BYTES),
        cost_estimate=conv_cost(state, rows),
        name="last_conv",
    )(state, above, below, water, held)


def conv_cost(state, rows):
    cells = rows * state.shape[1]
    width = state.shape[2]
    return pl.CostEstimate(
        flops=2 * 9 * cells * width * width,
        bytes_accessed=cells * width * 6 + 9 * width * width * 2,
        transcendentals=cells * width,
    )


def conv_inside(layer, begin, end, state, after, air_kernels, sea_kernels, keep):
    rows, cols, width = state.shape
    count = end - begin
    kernel_shape = air_kernels.shape[1:]
    scratch = [
        pltpu.VMEM(state.shape, BF16),
        pltpu.VMEM((count + 2, cols, 3 * width), BF16),
        pltpu.VMEM((count, cols, width), F32),
    ] + held_weights(air_kernels)
    scratch += [pltpu.SemaphoreType.DMA((2,)), pltpu.SemaphoreType.DMA((count // GROUP,))]
    if keep:
        scratch += held_weights(air_kernels) + [pltpu.SemaphoreType.DMA]
    return pl.pallas_call(
        functools.partial(inside_conv_kernel, layer, begin, end, keep),
        out_shape=(
            jax.ShapeDtypeStruct(state.shape, F32),
            jax.ShapeDtypeStruct(kernel_shape, BF16) if keep else jax.ShapeDtypeStruct((8, 128), F32),
        ),
        in_specs=[HBM] * 4,
        out_specs=(HBM, HBM if keep else VMEM),
        scratch_shapes=scratch,
        input_output_aliases={1: 0} if keep else {},
        compiler_params=params(),
        cost_estimate=conv_cost(state, count),
        name="conv_inside",
    )(state, after, air_kernels, sea_kernels)


EDGE_WEIGHTS = [(0, 0), (1, 0), (2, 0), (0, 2), (1, 2), (2, 2), (0, 1), (2, 1)]


def halo_columns(rows, left_ref, right_ref, weights, held, masked):
    before = silu(left_ref[...])
    after = silu(right_ref[...])
    half = before.shape[1] // 2
    if masked:
        before, after = before[:, half:], after[:, :half]
    west = jnp.zeros((rows, before.shape[1]), F32)
    east = jnp.zeros((rows, before.shape[1]), F32)
    size = before.shape[1]
    for d in range(3):
        if weights:
            weights[d, 0].wait()
        west = west + dot(before[d : d + rows].astype(BF16), held[d, 0, 0:size, 0:size])
    for d in range(3):
        if weights:
            weights[d, 2].wait()
        east = east + dot(after[d : d + rows].astype(BF16), held[d, 2, 0:size, 0:size])
    if masked:
        blank = jnp.zeros((rows, half), F32)
        west = jnp.concatenate([west, blank], axis=1)
        east = jnp.concatenate([blank, east], axis=1)
    return west, east


def side_kernel(
    out_in_hbm, sides_ref, left_ref, right_ref, water_ref, held, out_hbm, side_out, wide_water, turned, sems,
):
    del out_in_hbm
    rows, cols, width = out_hbm.shape
    half = width // 2
    writes = [
        pltpu.make_async_copy(side_out.at[k], out_hbm.at[:, pl.ds(start, BLOCK_COLS)], sems.at[k])
        for k, start in enumerate((0, cols - BLOCK_COLS))
    ]

    def run(_, make_line, product, masked):
        if masked:
            fill_water(water_ref, wide_water, turned)
        added = halo_columns(rows, left_ref, right_ref, None, held, masked)
        at = iota((BLOCK_COLS, width), 0)
        for k, (start, here) in enumerate(((0, 0), (cols - BLOCK_COLS, BLOCK_COLS - 1))):
            for r in range(rows):
                total = sides_ref[k, r] + jnp.where(at == here, added[k][r : r + 1], 0.0)
                if masked:
                    total = total * water_of_row(turned, rows, r, half, start, BLOCK_COLS)
                side_out[k, r] = total.astype(BF16)
            writes[k].start()

    each_component(run, None, None)
    for copy in writes:
        copy.wait()


def fix_sides(out, sides, beside, water, held):
    rows, cols, width = out.shape
    return pl.pallas_call(
        side_kernel,
        out_shape=jax.ShapeDtypeStruct(out.shape, BF16),
        in_specs=[HBM] + [VMEM] * 5,
        out_specs=HBM,
        scratch_shapes=[pltpu.VMEM((2, rows, BLOCK_COLS, width), BF16)]
        + water_scratch(cols)
        + [pltpu.SemaphoreType.DMA((2,))],
        input_output_aliases={0: 0},
        compiler_params=params(LATE_BYTES),
        name="fix_sides",
    )(out, sides, *beside, water, held)


def edge_copies(rows, cols, count, lines, sides, hbm, sems, inward):
    inner = pl.ds(1, rows - 2)
    pairs = [
        (lines.at[0], hbm.at[0]),
        (lines.at[1], hbm.at[rows - 1]),
        (sides.at[0], hbm.at[inner, pl.ds(0, count)]),
        (sides.at[1], hbm.at[inner, pl.ds(cols - count, count)]),
    ]
    return [
        pltpu.make_async_copy(*(pair[::-1] if inward else pair), sems.at[k]) for k, pair in enumerate(pairs)
    ]


SIDE = 8


def sum_edge_kernel(
    layer, sum_in_hbm, top_ref, bottom_ref, left_ref, right_ref, air_hbm, sea_hbm, sum_hbm,
    lines, sides, held, weight_sems, read_sems, sems,
):
    rows, cols, width = sum_hbm.shape
    reads = edge_copies(rows, cols, SIDE, lines, sides, sum_in_hbm, read_sems, True)
    writes = edge_copies(rows, cols, SIDE, lines, sides, sum_hbm, sems, False)
    for copy in reads:
        copy.start()

    def run(kernels_hbm, make_line, product, masked):
        size = width // 2 if masked else width
        weights = fetch_weights(layer, kernels_hbm, held, weight_sems, EDGE_WEIGHTS)
        none = jnp.zeros((1, width), F32)
        west, east = halo_columns(rows, left_ref, right_ref, weights, held, masked)
        for copy in reads:
            copy.wait()
        at = iota((SIDE, width), 0)
        for r in range(1, rows - 1):
            sides[0, r - 1] += jnp.where(at == 0, west[r : r + 1], 0.0)
            sides[1, r - 1] += jnp.where(at == SIDE - 1, east[r : r + 1], 0.0)
        at = iota((cols, width), 0)
        for k, (line, d) in enumerate(((top_ref, 0), (bottom_ref, 2))):
            r = 0 if k == 0 else rows - 1
            lined = make_line(silu(line[...].astype(F32)), none, none)
            weights[d, 1].wait()
            total = lines[k] + product(lined, held[d, :, 0:size, 0:size])
            total = total + jnp.where(at == 0, west[r : r + 1], 0.0)
            lines[k] = total + jnp.where(at == cols - 1, east[r : r + 1], 0.0)

    each_component(run, air_hbm, sea_hbm)
    for copy in writes:
        copy.start()
    for copy in writes:
        copy.wait()


def add_edges(layer, summed, halo, air_kernels, sea_kernels):
    rows, cols, width = summed.shape
    return pl.pallas_call(
        functools.partial(sum_edge_kernel, layer),
        out_shape=jax.ShapeDtypeStruct(summed.shape, F32),
        in_specs=[HBM] + [VMEM] * 4 + [HBM] * 2,
        out_specs=HBM,
        scratch_shapes=[
            pltpu.VMEM((2, cols, width), F32),
            pltpu.VMEM((2, rows - 2, SIDE, width), F32),
        ]
        + held_weights(air_kernels)
        + [pltpu.SemaphoreType.DMA((4,)), pltpu.SemaphoreType.DMA((4,))],
        input_output_aliases={0: 0},
        compiler_params=params(),
        name="add_edges",
    )(summed, *halo, air_kernels, sea_kernels)


def runs_of(block_rows, rows):
    runs = []
    for r in range(rows):
        if r % BLOCK_ROWS in block_rows:
            if runs and sum(runs[-1]) == r:
                runs[-1] = (runs[-1][0], runs[-1][1] + 1)
            else:
                runs.append((r, 1))
    return runs


def update_kernel(block_rows, last, *refs):
    if last:
        (labels_ref, message_hbm, sum_hbm, water_ref, coupling_hbm, early_new, above_ref, below_ref) = refs[:8]
        (early_left, early_right, new_ref, west_ref, east_ref) = refs[8:13]
        refs = refs[13:]
        left_ref, right_ref, refs = refs[0], refs[1], refs[2:]
    else:
        (labels_ref, message_hbm, sum_hbm, water_ref, coupling_hbm) = refs[:5]
        new_ref, top_ref, bottom_ref = refs[5:8]
        refs = refs[8:]
    (total, message, sum_ref, coupling_ref, wide_water, turned) = refs[:6]
    (message_sem, coupling_sem, sum_sems) = refs[6:]
    rows, cols, width = sum_ref.shape
    half = width // 2
    slots = message_hbm.shape[0] * SLOTS
    cells = len(block_rows) * BLOCK_COLS
    runs = runs_of(block_rows, rows)
    parts = [(start, count, block_rows.index(start)) for start, count in runs_of(block_rows, BLOCK_ROWS)]
    updated = [r for start, count in runs for r in range(start, start + count)]
    ocean = on_ocean()

    def run_copy(source, target, k, sems):
        at = pl.ds(*runs[k])
        return pltpu.make_async_copy(source.at[at], target.at[at], sems.at[k])

    message_copy = pltpu.make_async_copy(message_hbm, message, message_sem)
    coupling_copy = pltpu.make_async_copy(coupling_hbm, coupling_ref, coupling_sem)
    message_copy.start()
    for k in range(len(runs)):
        run_copy(sum_hbm, sum_ref, k, sum_sems).start()
    coupling_copy.start()
    if last:
        at = 0
        for start, count in runs_of([r for r in range(BLOCK_ROWS) if r not in block_rows], rows):
            new_ref[start : start + count] = early_new[at : at + count]
            at += count
        left_ref[...] = early_left[...]
        right_ref[...] = early_right[...]

    def clear(lanes):
        for start, count in runs:
            total[start : start + count, :, 0:lanes] = jnp.zeros((count, cols, lanes), F32)

    def each_slot(act):
        def one(s, _):
            label = labels_ref[s]

            @pl.when(label >= 0)
            def _():
                at = pl.multiple_of((s % SLOTS) * cells, BLOCK_COLS)
                act(message[s // SLOTS, pl.ds(at, cells), :].astype(F32), label)

            return 0

        lax.fori_loop(0, slots, one, 0)

    def store(r, line):
        low = line.astype(BF16)
        new_ref[r if last else updated.index(r)] = low
        if last:
            left_ref[r : r + 1] = low[:TILE].astype(F32)[:1]
            right_ref[r : r + 1] = low[cols - TILE :].astype(F32)[TILE - 1 :]
        elif r == 0:
            top_ref[...] = low
        elif r == rows - 1:
            bottom_ref[...] = low

    @pl.when(jnp.logical_not(ocean))
    def _():
        clear(half)
        across = cols // BLOCK_COLS

        def add(value, label):
            r0 = (label // across) * BLOCK_ROWS
            c0 = pl.multiple_of((label % across) * BLOCK_COLS, BLOCK_COLS)
            value = value.reshape(len(block_rows), BLOCK_COLS, half)
            for start, count, at in parts:
                total[pl.ds(r0 + start, count), pl.ds(c0, BLOCK_COLS), 0:half] += value[at : at + count]

        message_copy.wait()
        each_slot(add)
        coupling_copy.wait()
        for k, (start, count) in enumerate(runs):
            block = total[start : start + count, :, 0:half].astype(BF16).reshape(count * cols, half)
            force = dot(block, coupling_ref[...]).reshape(count, cols, width)
            run_copy(sum_hbm, sum_ref, k, sum_sems).wait()
            for q in range(count):
                store(start + q, sum_ref[start + q] + force[q])

    @pl.when(ocean)
    def _():
        clear(width)
        fill_water(water_ref, wide_water, turned)
        wide = BLOCK_COLS // 2
        across = cols // wide

        def add(value, label):
            r0 = (label // across) * BLOCK_ROWS
            c0 = pl.multiple_of((label % across) * wide, wide)
            value = value.reshape(2, len(block_rows), wide, half)
            for start, count, at in parts:
                for p in range(2):
                    lanes = slice(p * half, (p + 1) * half)
                    total[pl.ds(r0 + start, count), pl.ds(c0, wide), lanes] += value[p, at : at + count]

        message_copy.wait()
        each_slot(add)
        coupling_copy.wait()
        for k, (start, count) in enumerate(runs):
            run_copy(sum_hbm, sum_ref, k, sum_sems).wait()
            for r in range(start, start + count):
                store(r, (sum_ref[r] + total[r]) * water_of_row(turned, rows, r, half, 0, cols))

    if last:
        put_sides(above_ref, below_ref, left_ref, right_ref, west_ref, east_ref)


def update(block_rows, labels, message, summed, water, coupling_matrix, early=None):
    rows, cols, width = summed.shape
    last = early is not None
    side = jax.ShapeDtypeStruct((rows + 2, width), F32)
    runs = len(runs_of(block_rows, rows))
    count = rows if last else rows // BLOCK_ROWS * len(block_rows)
    kept = [pltpu.VMEM((rows, width), F32)] * 2 if last else []
    return pl.pallas_call(
        functools.partial(update_kernel, block_rows, last),
        out_shape=(jax.ShapeDtypeStruct((count, cols, width), BF16),)
        + ((side, side) if last else rim_shapes(rows, cols, width)[:2]),
        in_specs=[SMEM, HBM, HBM, VMEM, HBM] + ([VMEM] * 5 if last else []),
        out_specs=(VMEM,) * 3,
        scratch_shapes=kept
        + [
            pltpu.VMEM((rows, cols, width), F32),
            pltpu.VMEM(message.shape, BF16),
            pltpu.VMEM((rows, cols, width), F32),
            pltpu.VMEM(coupling_matrix.shape, BF16),
        ]
        + water_scratch(cols)
        + [
            pltpu.SemaphoreType.DMA,
            pltpu.SemaphoreType.DMA,
            pltpu.SemaphoreType.DMA((runs,)),
        ],
        compiler_params=params(UPDATE_BYTES if last else VMEM_BYTES),
        name="update",
    )(labels, message, summed, water, coupling_matrix, *(early or ()))


def early_sides_kernel(new_ref, _, __, left_ref, right_ref, ___):
    rows = left_ref.shape[0]
    cols = new_ref.shape[1]
    left_ref[...] = jnp.zeros_like(left_ref)
    right_ref[...] = jnp.zeros_like(right_ref)
    updated = [r for start, count in runs_of(SECOND, rows) for r in range(start, start + count)]
    for k, r in enumerate(updated):
        left_ref[r : r + 1] = new_ref[k, :TILE].astype(F32)[:1]
        right_ref[r : r + 1] = new_ref[k, cols - TILE :].astype(F32)[TILE - 1 :]


def early_sides(rows, new, summed, coupling_matrix):
    side = jax.ShapeDtypeStruct((rows, new.shape[2]), F32)
    return pl.pallas_call(
        early_sides_kernel,
        out_shape=(side, side, jax.ShapeDtypeStruct(summed.shape, F32)),
        in_specs=[VMEM, ANY, ANY],
        out_specs=(VMEM, VMEM, ANY),
        input_output_aliases={1: 2},
        compiler_params=params(LATE_BYTES),
        name="early_sides",
    )(new, summed, coupling_matrix)


def exchange(value, axis, bit):
    return lax.ppermute(value, axis, [(i, i ^ bit) for i in range(lax.axis_size(axis))])


def across_groups(value):
    return exchange(value, "grp", 1)


def to_owners(value):
    return lax.all_to_all(value, ("lat", "lon"), split_axis=0, concat_axis=0, tiled=True)


def rows_beside(top, bottom):
    lats = lax.axis_size("lat")
    above = lax.ppermute(bottom, "lat", [(i, i + 1) for i in range(lats - 1)])
    below = lax.ppermute(top, "lat", [(i + 1, i) for i in range(lats - 1)])
    return above, below


def columns_beside(west, east):
    lons = lax.axis_size("lon")
    before = lax.ppermute(east, "lon", [(i, (i + 1) % lons) for i in range(lons)])
    after = lax.ppermute(west, "lon", [((i + 1) % lons, i) for i in range(lons)])
    return before, after


def body(
    state,
    intersection_lists,
    intersection_matrices,
    water,
    air_kernels,
    sea_kernels,
    flux_projection,
    coupling_matrix,
):
    current = state[0]
    rows = current.shape[0]
    tiles = lax.axis_size("lat") * lax.axis_size("lon")
    entries = intersection_lists.shape[-1]
    matrices = intersection_matrices.reshape(entries, BLOCK, BLOCK)

    first, second, lists, top, bottom, left, right = payloads(
        intersection_lists, current, matrices, water, flux_projection, tiles
    )
    first = across_groups(first)
    second = to_owners(second)
    halo_rows = rows_beside(top, bottom)
    middle = rows // 2
    summed, token = conv_inside(0, 0, middle, current, left, air_kernels, sea_kernels, False)
    first, west, east = pack(tiles, across_groups(lists), first, *halo_rows, left, right, token)
    first = to_owners(first)
    second = across_groups(second)
    halo = halo_rows + columns_beside(west, east)
    summed, held = conv_inside(0, middle, rows, current, summed, air_kernels, sea_kernels, True)
    summed = add_edges(0, summed, halo, air_kernels, sea_kernels)

    labels = slot_labels(second)
    early, top, bottom = update(SECOND, labels, second, summed, water, coupling_matrix)
    halo_rows = rows_beside(top, bottom)
    left, right, summed = early_sides(rows, early, summed, coupling_matrix)
    current, west, east = update(
        FIRST, labels, first, summed, water, coupling_matrix, (early, *halo_rows, left, right)
    )
    beside = columns_beside(west, east)
    out, sides = last_conv(current, *halo_rows, water, held)
    out = fix_sides(out, sides, beside, water, held)
    return out[None]


def solution(mesh):
    placed = (
        P("grp", "lat", "lon", None),
        P("grp", "lat", "lon", None, None),
        P("grp", "lat", "lon", None, None, None),
        P("lat", "lon"),
        P(),
        P(),
        P(),
        P(),
    )
    return jax.shard_map(
        body, mesh=mesh, in_specs=placed, out_specs=P("grp", "lat", "lon", None), check_vma=False
    )
```
